256 devices in a mesh: dp: 32 (over z, y), tensor: 8 (over x, core).
Axes of the slice: x: 4, y: 4, z: 8, core: 2. Of those that a mesh axis runs over, the one named last changes fastest.
Arguments:
- gradients: bfloat16 [32, 64, 512, 512], P('dp', 'tensor')
- owners: int32 [8, 32], P('tensor'), may hold values from 0 to 31, each once within a row
- left_factor: float32 [8, 32, 512, 512], P('tensor', 'dp')
- right_factor: float32 [8, 32, 512, 512], P('tensor', 'dp')
- left_root: bfloat16 [8, 32, 512, 512], P('tensor', 'dp')
- right_root: bfloat16 [8, 32, 512, 512], P('tensor', 'dp')
Outputs:
- new_left: float32 [8, 32, 512, 512], P('tensor', 'dp')
- new_right: float32 [8, 32, 512, 512], P('tensor', 'dp')
- directions: bfloat16 [64, 512, 512], P('tensor', 'dp')
The draws below stay inside these ranges and needn't reach their ends.
Inputs may be any that keep to these rules, and one draw needn't show every extreme that they name: Each row of owners is a permutation of the replica indices; block j < 8 of tensor shard t is owned by replica owners[t, j], the replicas in the other entries own no block.
All inputs are finite; a program needn't handle non-finite values.
Results may differ from the reference program's by a relative error of at most 0.025.
Values may be sent and summed in bfloat16 or wider, within the bound.
A program may use at most 128 MiB of HBM per device.

```python
import math
import jax
import jax.numpy as jnp
from jax import lax

B = 512
BLK_TP = 8
N_DP = 32
N_TENSOR = 8


def symmetric_draw(raw_noise, diag_key, noise_scale, diag_low, diag_high):
    sym_part = 0.5 * (raw_noise + jnp.swapaxes(raw_noise, -1, -2)) * noise_scale
    diag_values = jnp.exp(jax.random.uniform(diag_key, raw_noise.shape[:-1], jnp.float32, math.log(diag_low), math.log(diag_high)))
    identity = jnp.eye(raw_noise.shape[-1], dtype=jnp.float32)
    return sym_part + identity * diag_values[..., None, :]


def draw_gradients(key, part):
    key = jax.random.fold_in(key, 11)
    keys = jax.random.split(key, 5)
    block_total = N_TENSOR * BLK_TP
    shape = (N_DP, block_total, B, B)
    raw = jnp.clip(jax.random.normal(keys[0], shape, jnp.float32), -6.0, 6.0)
    row_scale = jnp.exp(jax.random.uniform(keys[1], (1, block_total, B, 1), jnp.float32, math.log(0.3), math.log(3.0)))
    col_scale = jnp.exp(jax.random.uniform(keys[2], (1, block_total, 1, B), jnp.float32, math.log(0.3), math.log(3.0)))
    ramp = jnp.exp(math.log(3.0) * jnp.arange(block_total, dtype=jnp.float32) / max(block_total - 1, 1))
    ramp = ramp * jax.random.uniform(keys[3], (block_total,), jnp.float32, 0.7, 1.4)
    replica = jax.random.uniform(keys[4], (N_DP, 1, 1, 1), jnp.float32, 0.5, 2.0) / math.sqrt(N_DP)
    return (raw * row_scale * col_scale * ramp.reshape(1, block_total, 1, 1) * replica).astype(jnp.bfloat16)


def draw_left_factor(key, part):
    key = jax.random.fold_in(key, 21)
    first, second = jax.random.split(key)
    raw = jax.random.normal(first, (N_TENSOR, N_DP, B, B), jnp.float32)
    return symmetric_draw(raw, second, 1.0, 1.0, 3.0)


def draw_right_factor(key, part):
    key = jax.random.fold_in(key, 22)
    first, second = jax.random.split(key)
    raw = jax.random.normal(first, (N_TENSOR, N_DP, B, B), jnp.float32)
    return symmetric_draw(raw, second, 1.0, 1.0, 3.0)


def draw_left_root(key, part):
    key = jax.random.fold_in(key, 23)
    first, second = jax.random.split(key)
    raw = jax.random.normal(first, (N_TENSOR, N_DP, B, B), jnp.float32)
    return symmetric_draw(raw, second, 0.5 / math.sqrt(B), 0.5, 2.0).astype(jnp.bfloat16)


def draw_right_root(key, part):
    key = jax.random.fold_in(key, 24)
    first, second = jax.random.split(key)
    raw = jax.random.normal(first, (N_TENSOR, N_DP, B, B), jnp.float32)
    return symmetric_draw(raw, second, 0.5 / math.sqrt(B), 0.5, 2.0).astype(jnp.bfloat16)


def setup_inputs(seed: int = 0) -> dict:
    splits = jax.random.split(jax.random.key(seed), 7)
    return {
        "gradients": draw_gradients(jax.random.fold_in(splits[6], 71), 0),
        "owners": jax.vmap(lambda own: jax.random.permutation(own, N_DP))(jax.random.split(splits[1], N_TENSOR)).reshape((N_TENSOR, N_DP)).astype(jnp.int32),
        "left_factor": draw_left_factor(jax.random.fold_in(splits[6], 71), 0),
        "right_factor": draw_right_factor(jax.random.fold_in(splits[6], 71), 0),
        "left_root": draw_left_root(jax.random.fold_in(splits[6], 71), 0),
        "right_root": draw_right_root(jax.random.fold_in(splits[6], 71), 0),
    }


decay_rate = 0.95
epsilon = 1e-06

def reference(gradients, owners, left_factor, right_factor, left_root, right_root):
    block_total = N_TENSOR * BLK_TP
    owner_of = owners[:, :BLK_TP].reshape(block_total).astype(jnp.int32)
    column_of = (jnp.arange(block_total) // BLK_TP).astype(jnp.int32)
    gram_weight = (1.0 - decay_rate) / B

    def per_block(block_id):
        column = column_of[block_id]
        owner = owner_of[block_id]
        grad_sum = lax.optimization_barrier(jnp.sum(gradients[:, block_id].astype(jnp.float32), axis=0))
        grad_block = grad_sum.astype(jnp.bfloat16)
        left_gram = jnp.dot(grad_block, grad_block.T, preferred_element_type=jnp.float32)
        right_gram = jnp.dot(grad_block.T, grad_block, preferred_element_type=jnp.float32)
        half_way = jnp.dot(left_root[column, owner], grad_block, preferred_element_type=jnp.float32).astype(jnp.bfloat16)
        precond = jnp.dot(half_way, right_root[column, owner], preferred_element_type=jnp.float32)
        shaped = precond * jnp.sqrt(jnp.mean(grad_sum * grad_sum) + epsilon) / jnp.sqrt(jnp.mean(precond * precond) + epsilon)
        return (left_gram, right_gram, shaped, jnp.sum(shaped * shaped))
    left_gram, right_gram, shaped, squares = lax.map(per_block, jnp.arange(block_total).astype(jnp.int32))
    new_left = (decay_rate * left_factor).at[column_of, owner_of].add(gram_weight * left_gram)
    new_right = (decay_rate * right_factor).at[column_of, owner_of].add(gram_weight * right_gram)
    global_sum = jnp.sum(squares)
    scale = 1.0 / jnp.sqrt(global_sum / (block_total * B * B) + epsilon)
    directions = (shaped * scale).astype(jnp.bfloat16)
    return (new_left, new_right, directions)
```

```python
import functools

import jax
import jax.numpy as jnp
from jax import lax
from jax.experimental import pallas as pl
from jax.experimental.pallas import tpu as pltpu
from jax.sharding import PartitionSpec as P

MESH = pl.DeviceIdType.MESH
F32 = jnp.float32
BF16 = jnp.bfloat16
decay_rate = 0.95
epsilon = 1e-06
NY = 4

ROUNDS = (
    (0, 256, (3, 3, 1, 1)),
    (256, 256, (3, 2, 1, 2)),
)


def sets_of(counts):
    at, found = 0, []
    for nb, (yfirst, s) in zip(counts, ((True, 1), (True, -1), (False, 1), (False, -1))):
        if nb:
            found.append((at, nb, yfirst, s))
        at += nb
    return found


def plan(events, rate=0.18, latency=1.5, lead=2.0):
    free = dict.fromkeys(("y1", "y-1", "z1", "z-1"), 0.0)
    arrive, done, order, now = {}, {}, [], 0.0
    left = list(events)
    while left:
        best = None
        for e in left:
            if any(m not in arrive for m in e["needs"]) or any(d not in done for d in e["after"]):
                continue
            ready = max([arrive[m] for m in e["needs"]] + [now])
            if not e["needs"] and not e["after"]:
                ready = max([now] + [free[link] - lead for _, link, _ in e["sends"]])
            key = (ready, e["rank"])
            if best is None or key < best[0]:
                best = (key, e)
        (ready, _), e = best
        now = ready + e["cost"]
        for name, link, kib in e["sends"]:
            free[link] = max(free[link], now) + kib * 1.024 / 100 * 2 / 0.9
            arrive[name] = free[link] + latency
        done[e["name"]] = now
        order.append(e)
        left.remove(e)
    return order, now


def per_device(nz, n_tensor, gradients, owners, left_factor, right_factor, left_root, right_root):
    nb_all, width = gradients.shape[1], gradients.shape[2]
    n_dp = nz * NY
    strip = width // n_dp
    g = gradients.reshape(nb_all, nz, NY, strip, width)
    sets = [(k, c0, w) + s for k, (c0, w, counts) in enumerate(ROUNDS) for s in sets_of(counts)]
    names, shapes = [], []

    def buffer(name, shape, dtype=BF16):
        names.append(name)
        shapes.append(pltpu.VMEM(shape, dtype))

    messages = {}
    for i, (k, c0, w, b0, nb, yfirst, s) in enumerate(sets):
        ychunk = (nb, nz, strip, w) if yfirst else (nb, strip, w)
        zchunk = (nb, strip, w) if yfirst else (nb, NY, strip, w)
        for n in ("ry1", "ry2", "ry3", "sy"):
            buffer(f"{n}_{i}", ychunk)
        buffer(f"mid_{i}", ychunk if yfirst else zchunk)
        half = nz // 2
        buffer(f"rza_{i}", (half,) + zchunk)
        buffer(f"rzb_{i}", (half - 1,) + zchunk)
        buffer(f"sza_{i}", (half - 1,) + zchunk)
        buffer(f"szb_{i}", (half - 2,) + zchunk)
        for n in ["y1", "y2", "y3"] + [f"a{h}" for h in range(half)] + [f"b{h}" for h in range(half - 1)]:
            messages[f"{n}_{i}"] = len(messages)
    for k, (c0, w, _) in enumerate(ROUNDS):
        buffer(f"agg_{k}", (nb_all, strip, w))
        buffer(f"stage_{k}", (n_dp, strip, w))
        buffer(f"grad_{k}", (n_dp, strip, w))
    buffer("own", (nb_all, nz, NY, strip, width))
    buffer("lroot", (width, width))
    buffer("rroot", (width, width))
    buffer("lfac", (width, width), F32)
    buffer("rfac", (width, width), F32)
    buffer("pre", (width, width), F32)
    buffer("shaped", (n_dp, strip, width))
    buffer("arrived", (n_dp, strip, width))
    buffer("sum_t", (n_tensor, 8, 128), F32)
    buffer("sum_y", (NY, 8, 128), F32)
    buffer("sum_z", (nz, 8, 128), F32)

    n_msg = len(messages)
    n_rounds = len(ROUNDS)

    def kernel(owners_ref, g_ref, lf_ref, rf_ref, lr_ref, rr_ref, nl_ref, nr_ref, dir_ref, *scratch):
        buf = dict(zip(names, scratch))
        send, recv, own_sem, load_sem, a2a_send, a2a_recv, sum_send, sum_recv, out_sem = scratch[len(names):]
        me, ten = lax.axis_index("dp"), lax.axis_index("tensor")
        z, y = me // NY, me % NY

        def zat(d):
            return lax.rem(z + d + 2 * nz, nz)

        def yat(d):
            return lax.rem(y + d + 2 * NY, NY)

        def zdev(d):
            return (zat(d) * NY + y, ten)

        def ydev(d):
            return (z * NY + yat(d), ten)

        barrier = pltpu.get_barrier_semaphore()

        def greet(o, _):
            pl.semaphore_signal(barrier, inc=1, device_id=(lax.rem(me + o, n_dp), ten), device_id_type=MESH)
            return 0

        lax.fori_loop(1, n_dp, greet, 0)
        for o in range(1, n_tensor):
            pl.semaphore_signal(barrier, inc=1, device_id=(me, lax.rem(ten + o, n_tensor)), device_id_type=MESH)
        pl.semaphore_wait(barrier, n_dp - 1 + n_tensor - 1)

        own_copies = []
        for k, (c0, w, _) in enumerate(ROUNDS):
            cols = pl.ds(c0, w)
            own_copies.append(
                pltpu.make_async_copy(
                    g_ref.at[:, :, :, :, cols], buf["own"].at[:, :, :, :, cols], own_sem.at[k]
                )
            )
        loads = [
            pltpu.make_async_copy(lr_ref, buf["lroot"], load_sem.at[0]),
            pltpu.make_async_copy(rr_ref, buf["rroot"], load_sem.at[1]),
            pltpu.make_async_copy(lf_ref, buf["lfac"], load_sem.at[2]),
            pltpu.make_async_copy(rf_ref, buf["rfac"], load_sem.at[3]),
        ]
        copies = {}

        def put(name, src, dst, dev):
            i = messages[name]
            copies[name] = pltpu.make_async_remote_copy(
                src_ref=src, dst_ref=dst, send_sem=send.at[i], recv_sem=recv.at[i],
                device_id=dev, device_id_type=MESH,
            )
            copies[name].start()

        def total(parts):
            if len(parts) == 2:
                return parts[0] + parts[1]
            acc = parts[0].astype(F32)
            for p in parts[1:]:
                acc = acc + p.astype(F32)
            return acc.astype(BF16)

        events = []

        def event(name, emit, rank, needs=(), after=(), sends=(), cost=0.2):
            events.append(dict(name=name, emit=emit, rank=rank, needs=needs, after=after, sends=sends, cost=cost))

        loaded = set()

        def need_own(k):
            if k not in loaded:
                loaded.add(k)
                own_copies[k].wait()

        half = nz // 2
        finals = {k: [] for k in range(n_rounds)}
        for i, (k, c0, w, b0, nb, yfirst, s) in enumerate(sets):
            cols = pl.ds(c0, w)
            blocks = pl.ds(b0, nb)
            kib = nb * strip * w * 2 / 1024

            def own_y(src, i=i, blocks=blocks, cols=cols, yfirst=yfirst):
                return (lambda d: src.at[blocks, :, yat(d), :, cols]) if yfirst else (lambda d: src.at[:, yat(d)])

            def own_z(src, i=i, blocks=blocks, cols=cols, yfirst=yfirst):
                return (lambda d: src.at[:, zat(d)]) if yfirst else (lambda d: src.at[blocks, zat(d), :, :, cols])

            def fold(dst, parts, lead, n_lead, nb=nb):
                if not lead:
                    for b in range(nb):
                        dst[b] = total([p[b] for p in parts])
                    return

                def one(v, _):
                    for b in range(nb):
                        dst[b, v] = total([p[b, v] for p in parts])
                    return 0

                lax.fori_loop(0, n_lead, one, 0)

            first_y, first_z = yfirst, not yfirst
            ysize = kib * nz if yfirst else kib
            zsize = kib if yfirst else kib * NY
            mid = buf[f"mid_{i}"]
            y_raw = own_y(g_ref if yfirst else mid)
            y_own = own_y(buf["own"] if yfirst else mid)
            z_raw = own_z(mid if yfirst else g_ref)
            z_own = own_z(mid if yfirst else buf["own"])
            agg = buf[f"agg_{k}"].at[blocks]
            ry1, ry2, ry3, sy = (buf[f"{n}_{i}"] for n in ("ry1", "ry2", "ry3", "sy"))
            rza, rzb, sza, szb = (buf[f"{n}_{i}"] for n in ("rza", "rzb", "sza", "szb"))
            ylead = (yfirst, nz)
            zlead = (not yfirst, NY)
            up, down = s, -s
            yl, zl = {1: f"y{s}", -1: f"y{-s}"}, {1: f"z{s}", -1: f"z{-s}"}
            yk = k * 10 + (0 if yfirst else 5)
            zk = k * 10 + (5 if yfirst else 0)
            ybase = () if yfirst else (f"zdone_{i}",)
            zbase = (f"ydone_{i}",) if yfirst else ()

            def y0(i=i, y_raw=y_raw, ry1=ry1, ry3=ry3, s=s):
                put(f"y1_{i}", y_raw(2 * s), ry1, ydev(s))
                put(f"y3_{i}", y_raw(-s), ry3, ydev(-s))

            def y1(i=i, k=k, y_own=y_own, ry1=ry1, ry2=ry2, sy=sy, s=s, fold=fold, ylead=ylead):
                need_own(k)
                copies[f"y1_{i}"].wait_recv()
                fold(sy, [ry1, y_own(s)], *ylead)
                put(f"y2_{i}", sy, ry2, ydev(s))

            def y2(i=i, k=k, y_own=y_own, ry2=ry2, ry3=ry3, fold=fold, ylead=ylead,
                   dst=mid if yfirst else agg):
                need_own(k)
                copies[f"y2_{i}"].wait_recv()
                copies[f"y3_{i}"].wait_recv()
                fold(dst, [ry2, ry3, y_own(0)], *ylead)

            event(f"y0_{i}", y0, yk, after=ybase,
                  sends=[(f"y1_{i}", yl[1], ysize), (f"y3_{i}", yl[-1], ysize)])
            event(f"y1_{i}", y1, yk - 1, needs=[f"y1_{i}"], sends=[(f"y2_{i}", yl[1], ysize)])
            event(f"ydone_{i}", y2, yk - 2, needs=[f"y2_{i}", f"y3_{i}"])

            def zstart(i=i, z_raw=z_raw, rza=rza, rzb=rzb, s=s):
                put(f"a0_{i}", z_raw(half * s), rza.at[0], zdev(s))
                put(f"b0_{i}", z_raw(-(half - 1) * s), rzb.at[0], zdev(-s))

            event(f"z0_{i}", zstart, zk, after=zbase,
                  sends=[(f"a0_{i}", zl[1], zsize), (f"b0_{i}", zl[-1], zsize)])
            for h in range(1, half):
                def za(i=i, k=k, h=h, z_own=z_own, rza=rza, sza=sza, s=s, fold=fold, zlead=zlead):
                    need_own(k)
                    copies[f"a{h - 1}_{i}"].wait_recv()
                    fold(sza.at[h - 1], [rza.at[h - 1], z_own((half - h) * s)], *zlead)
                    put(f"a{h}_{i}", sza.at[h - 1], rza.at[h], zdev(s))

                event(f"za{h}_{i}", za, zk - 1, needs=[f"a{h - 1}_{i}"], sends=[(f"a{h}_{i}", zl[1], zsize)])
            for h in range(1, half - 1):
                def zb(i=i, k=k, h=h, z_own=z_own, rzb=rzb, szb=szb, s=s, fold=fold, zlead=zlead):
                    need_own(k)
                    copies[f"b{h - 1}_{i}"].wait_recv()
                    fold(szb.at[h - 1], [rzb.at[h - 1], z_own(-(half - 1 - h) * s)], *zlead)
                    put(f"b{h}_{i}", szb.at[h - 1], rzb.at[h], zdev(-s))

                event(f"zb{h}_{i}", zb, zk - 1, needs=[f"b{h - 1}_{i}"], sends=[(f"b{h}_{i}", zl[-1], zsize)])

            def zend(i=i, k=k, z_own=z_own, rza=rza, rzb=rzb, fold=fold, zlead=zlead,
                     dst=agg if yfirst else mid):
                need_own(k)
                copies[f"a{half - 1}_{i}"].wait_recv()
                copies[f"b{half - 2}_{i}"].wait_recv()
                fold(dst, [rza.at[half - 1], rzb.at[half - 2], z_own(0)], *zlead)

            event(f"zdone_{i}", zend, zk - 2, needs=[f"a{half - 1}_{i}", f"b{half - 2}_{i}"])
            finals[k].append(f"zdone_{i}" if yfirst else f"ydone_{i}")

        def block_of(device):
            found = jnp.int32(0)
            for j in range(nb_all):
                found = jnp.where(owners_ref[0, j] == device, j, found)
            return found

        def peer(o):
            dz, dy = o // NY, o % NY
            step = jnp.where(dz % 2 == 1, (dz + 1) // 2, nz - dz // 2)
            return lax.rem(z + step, nz) * NY + lax.rem(y + dy, NY)

        for k, (c0, w, _) in enumerate(ROUNDS):
            kib = strip * w * 2 / 1024

            def route(k=k):
                agg, stage, grad = (buf[f"{n}_{k}"] for n in ("agg", "stage", "grad"))

                def one(o, _):
                    to = peer(o)
                    stage[o] = agg[block_of(to)]
                    pltpu.make_async_remote_copy(
                        src_ref=stage.at[o], dst_ref=grad.at[me], send_sem=a2a_send.at[k], recv_sem=a2a_recv.at[k],
                        device_id=(to, ten), device_id_type=MESH,
                    ).start()
                    return 0

                lax.fori_loop(1, n_dp, one, 0)
                grad[me] = agg[block_of(me)]

            event(f"route_{k}", route, k * 10 - 3, after=finals[k],
                  sends=[(f"rz{q}_{k}", f"z{q}", kib * 8 * NY) for q in (1, -1)]
                  + [(f"ry{q}_{k}", f"y{q}", kib * 2 * nz) for q in (1, -1)], cost=1.0)

        for c in own_copies:
            c.start()
        order, _ = plan(events)
        n_first = 0
        started = False
        for e in order:
            if not started and e["needs"]:
                started = True
                for c in loads:
                    c.start()
            e["emit"]()

        def a2a_all(sem, ref):
            part = ref.at[pl.ds(0, n_dp - 1)]
            return pltpu.make_async_copy(part, part, sem)

        for k in range(n_rounds):
            a2a_all(a2a_recv.at[k], buf[f"grad_{k}"]).wait()
        for c in loads:
            c.wait()

        def whole():
            parts = [buf[f"grad_{k}"][...].reshape(width, ROUNDS[k][1]) for k in range(n_rounds)]
            return parts[0] if len(parts) == 1 else jnp.concatenate(parts, axis=1)

        owned = jnp.int32(0)
        for j in range(nb_all):
            owned = owned + jnp.where(owners_ref[0, j] == me, 1, 0)
        mine = owned > 0
        grad = whole()
        tall = 128
        pre = buf["pre"]
        squares = jnp.zeros((8, width), F32)
        for i in range(width // tall):
            rows = pl.ds(i * tall, tall)
            half_way = jnp.dot(buf["lroot"][rows, :], grad, preferred_element_type=F32).astype(BF16)
            p = jnp.dot(half_way, buf["rroot"][...], preferred_element_type=F32)
            pre[rows, :] = p
            squares = squares + jnp.sum((p * p).reshape(tall // 8, 8, width), axis=0)
        gf = grad.astype(F32)
        grad_squares = jnp.sum((gf * gf).reshape(width // 8, 8, width), axis=0)
        count = width * width
        grad_mean = jnp.sum(grad_squares, axis=(0, 1), keepdims=True) / count
        pre_mean = jnp.sum(squares, axis=(0, 1), keepdims=True) / count
        factor = jnp.sqrt(grad_mean + epsilon) / jnp.sqrt(pre_mean + epsilon)
        for i in range(width // tall):
            rows = pl.ds(i * tall, tall)
            per = tall // strip
            shaped = (pre[rows, :] * factor).astype(BF16)
            buf["shaped"][pl.ds(i * per, per)] = shaped.reshape(per, strip, width)

        shaped, arrived = buf["shaped"], buf["arrived"]

        def give(o, _):
            to = peer(o)
            pltpu.make_async_remote_copy(
                src_ref=shaped.at[to], dst_ref=arrived.at[me], send_sem=a2a_send.at[n_rounds],
                recv_sem=a2a_recv.at[n_rounds], device_id=(to, ten), device_id_type=MESH,
            ).start()
            return 0

        local = (pre_mean / (pre_mean + epsilon)) * (grad_mean + epsilon) * count
        local = lax.select(mine, local, jnp.zeros_like(local))
        local = jnp.broadcast_to(local, (8, 128))

        def exchange(ref, n, dev, at, value):
            ref[0] = value
            if n == 1:
                return value
            for o in range(1, n):
                pltpu.make_async_remote_copy(
                    src_ref=ref.at[0], dst_ref=ref.at[o], send_sem=sum_send.at[at], recv_sem=sum_recv.at[at],
                    device_id=dev(o), device_id_type=MESH,
                ).start()

            def finish():
                part = ref.at[pl.ds(1, n - 1)]
                pltpu.make_async_copy(part, part, sum_recv.at[at]).wait()
                return jnp.sum(ref[...], axis=0)

            return finish

        finish = exchange(buf["sum_t"], n_tensor, lambda o: (me, lax.rem(ten + o, n_tensor)), 0, local)
        lax.fori_loop(1, n_dp, give, 0)
        arrived[me] = shaped[me]

        gram_weight = (1.0 - decay_rate) / width

        def statistic(factor_ref, gram):
            add = gram_weight * gram
            add = lax.select(mine, add, jnp.zeros_like(add))
            return decay_rate * factor_ref + add

        for i in range(width // tall):
            rows = pl.ds(i * tall, tall)
            gram = jnp.zeros((tall, width), F32)
            for k in range(n_rounds):
                gk = buf[f"grad_{k}"]
                per = tall // strip
                top = gk[pl.ds(i * per, per)].reshape(tall, ROUNDS[k][1])
                gram = gram + lax.dot_general(top, gk[...].reshape(width, ROUNDS[k][1]), (((1,), (1,)), ((), ())),
                                              preferred_element_type=F32)
            buf["lfac"][rows, :] = statistic(buf["lfac"][rows, :], gram)
        out_left = pltpu.make_async_copy(buf["lfac"], nl_ref, out_sem.at[0])
        out_left.start()
        if n_tensor > 1:
            local = finish()
        finish = exchange(buf["sum_y"], NY, lambda o: (z * NY + lax.rem(y + o, NY), ten), 1, local)
        flipped = grad.T
        for i in range(width // tall):
            rows = pl.ds(i * tall, tall)
            gram = jnp.dot(flipped[i * tall:(i + 1) * tall], grad, preferred_element_type=F32)
            buf["rfac"][rows, :] = statistic(buf["rfac"][rows, :], gram)
        out_right = pltpu.make_async_copy(buf["rfac"], nr_ref, out_sem.at[1])
        out_right.start()
        local = finish()
        finish = exchange(buf["sum_z"], nz, lambda o: (lax.rem(z + o, nz) * NY + y, ten), 2, local)
        local = finish()
        entries = nb_all * n_tensor * width * width
        scale = 1.0 / jnp.sqrt(local / entries + epsilon)
        scale = jnp.broadcast_to(scale[0:1, 0:1], (strip, width))
        a2a_all(a2a_recv.at[n_rounds], arrived).wait()
        for j in range(nb_all):
            dir_ref[j] = (arrived[owners_ref[0, j]].astype(F32) * scale).astype(BF16)

        for c in copies.values():
            c.wait_send()
        for k in range(n_rounds):
            a2a_all(a2a_send.at[k], buf[f"stage_{k}"]).wait()
        a2a_all(a2a_send.at[n_rounds], shaped).wait()
        for at, (n, ref) in enumerate(((n_tensor, buf["sum_t"]), (NY, buf["sum_y"]), (nz, buf["sum_z"]))):
            if n > 1:
                part = ref.at[pl.ds(1, n - 1)]
                pltpu.make_async_copy(part, part, sum_send.at[at]).wait()
        out_left.wait()
        out_right.wait()

    hbm = pl.BlockSpec(memory_space=pl.ANY)
    vmem = pl.BlockSpec(memory_space=pltpu.VMEM)
    new_left, new_right, directions = pl.pallas_call(
        kernel,
        out_shape=(
            jax.ShapeDtypeStruct((width, width), F32),
            jax.ShapeDtypeStruct((width, width), F32),
            jax.ShapeDtypeStruct((nb_all, strip, width), BF16),
        ),
        in_specs=[pl.BlockSpec(memory_space=pltpu.SMEM)] + [hbm] * 5,
        out_specs=(hbm, hbm, vmem),
        scratch_shapes=shapes
        + [
            pltpu.SemaphoreType.DMA((n_msg,)),
            pltpu.SemaphoreType.DMA((n_msg,)),
            pltpu.SemaphoreType.DMA((n_rounds,)),
            pltpu.SemaphoreType.DMA((4,)),
            pltpu.SemaphoreType.DMA((n_rounds + 1,)),
            pltpu.SemaphoreType.DMA((n_rounds + 1,)),
            pltpu.SemaphoreType.DMA((3,)),
            pltpu.SemaphoreType.DMA((3,)),
            pltpu.SemaphoreType.DMA((2,)),
        ],
        compiler_params=pltpu.CompilerParams(
            collective_id=0, has_side_effects=True, vmem_limit_bytes=48 * 1024 * 1024
        ),
        name="shampoo",
    )(owners, g, left_factor[0, 0], right_factor[0, 0], left_root[0, 0], right_root[0, 0])
    return new_left[None, None], new_right[None, None], directions


def solution(mesh):
    nz = mesh.shape["dp"] // NY
    return jax.shard_map(
        functools.partial(per_device, nz, mesh.shape["tensor"]),
        mesh=mesh,
        in_specs=(
            P("dp", "tensor", None, None),
            P("tensor", None),
            P("tensor", "dp", None, None),
            P("tensor", "dp", None, None),
            P("tensor", "dp", None, None),
            P("tensor", "dp", None, None),
        ),
        out_specs=(
            P("tensor", "dp", None, None),
            P("tensor", "dp", None, None),
            P("tensor", "dp", None),
        ),
        check_vma=False,
    )
```

```python
import functools

import jax
import jax.numpy as jnp
from jax import lax
from jax.experimental import pallas as pl
from jax.experimental.pallas import tpu as pltpu
from jax.sharding import PartitionSpec as P

MESH = pl.DeviceIdType.MESH
F32 = jnp.float32
BF16 = jnp.bfloat16
decay_rate = 0.95
epsilon = 1e-06
NY = 4

ROUNDS = (
    (0, 256, ((3, "y", 1, "cd"), (3, "y", -1, "cd"), (1, "z", 1, "cd"), (1, "z", -1, "cd"))),
    (256, 256, ((2, "y", 1, "cd"), (2, "y", -1, "cd"), (2, "z", 1, "cd"), (2, "z", -1, "cd"))),
)
FULL = False
FOLD = 0.002
YFAR = (1, -1, 2)
ZFAR = (1, -1, 2, -2, 3, -3, 4)
MODEL = (46.5, 2.2, 3.0)


class Whole:
    def __init__(self, ref, send, recv):
        self.ref, self.send, self.recv = ref, send, recv

    def wait_recv(self):
        pltpu.make_async_copy(self.ref, self.ref, self.recv).wait()

    def wait_send(self):
        pltpu.make_async_copy(self.ref, self.ref, self.send).wait()


def plan(events, rate, latency, lead):
    free = dict.fromkeys(("y1", "y-1", "z1", "z-1"), 0.0)
    arrive, done, order, now = {}, {}, [], 0.0
    left = list(events)
    while left:
        best = None
        for e in left:
            if any(m not in arrive for m in e["needs"]) or any(d not in done for d in e["after"]):
                continue
            ready = max([arrive[m] for m in e["needs"]] + [now])
            if not e["needs"] and not e["after"]:
                ready = max([now] + [free[link] - lead for _, link, _ in e["sends"]])
            key = (ready, e["rank"])
            if best is None or key < best[0]:
                best = (key, e)
        (ready, _), e = best
        now = ready + e["cost"]
        for name, link, kib in e["sends"]:
            free[link] = max(free[link], now) + kib * 1.024 / rate
            arrive[name] = free[link] + latency
        done[e["name"]] = now
        order.append(e)
        left.remove(e)
    return order, now


def per_device(nz, n_tensor, gradients, owners, left_factor, right_factor, left_root, right_root):
    nb_all, width = gradients.shape[1], gradients.shape[2]
    n_dp = nz * NY
    strip = width // n_dp
    g = gradients.reshape(nb_all, nz, NY, strip, width)
    sets = []
    for k, (c0, w, found) in enumerate(ROUNDS):
        b0 = 0
        for nb, axis, s, forms in found:
            sets.append((k, c0, w, b0, nb, axis == "y", s, forms))
            b0 += nb
    names, shapes = [], []

    def buffer(name, shape, dtype=BF16):
        names.append(name)
        shapes.append(pltpu.VMEM(shape, dtype))

    messages = {}
    half = nz // 2
    for i, (k, c0, w, b0, nb, yfirst, s, forms) in enumerate(sets):
        ychunk = (nb, nz, strip, w) if yfirst else (nb, strip, w)
        zchunk = (nb, strip, w) if yfirst else (nb, NY, strip, w)
        yform, zform = forms if yfirst else forms[::-1]
        buffer(f"mid_{i}", ychunk if yfirst else zchunk)
        if yform == "c":
            for n in ("ry1", "ry2", "ry3", "sy"):
                buffer(f"{n}_{i}", ychunk)
            found = ["y1", "y2", "y3"]
        else:
            buffer(f"ry_{i}", (NY - 1,) + ychunk)
            found = ["y"]
        if zform == "c":
            buffer(f"rza_{i}", (half,) + zchunk)
            buffer(f"rzb_{i}", (half - 1,) + zchunk)
            buffer(f"sza_{i}", (half - 1,) + zchunk)
            buffer(f"szb_{i}", (half - 2,) + zchunk)
            found += [f"a{h}" for h in range(half)] + [f"b{h}" for h in range(half - 1)]
        else:
            buffer(f"rz_{i}", (nz - 1,) + zchunk)
            found += ["z"]
        for n in found:
            messages[f"{n}_{i}"] = len(messages)
    for k, (c0, w, _) in enumerate(ROUNDS):
        buffer(f"agg_{k}", (nb_all, strip, w))
        buffer(f"stage_{k}", (n_dp, strip, w))
        buffer(f"grad_{k}", (n_dp, strip, w))
    buffer("own", (nb_all, nz, NY, strip, width))
    buffer("lroot", (width, width))
    buffer("rroot", (width, width))
    buffer("lfac", (width, width), F32)
    buffer("rfac", (width, width), F32)
    buffer("pre", (width, width), F32)
    buffer("half", (width, width))
    buffer("gsq", (len(ROUNDS), 8, 128), F32)
    buffer("shaped", (n_dp, strip, width))
    buffer("arrived", (n_dp, strip, width))
    buffer("sum_t", (n_tensor, 8, 128), F32)
    buffer("sum_y", (NY, 8, 128), F32)
    buffer("sum_z", (nz, 8, 128), F32)

    n_msg = len(messages)
    n_rounds = len(ROUNDS)

    def kernel(owners_ref, g_ref, lf_ref, rf_ref, lr_ref, rr_ref, nl_ref, nr_ref, dir_ref, *scratch):
        buf = dict(zip(names, scratch))
        send, recv, own_sem, load_sem, a2a_send, a2a_recv, sum_send, sum_recv = scratch[len(names):]
        me, ten = lax.axis_index("dp"), lax.axis_index("tensor")
        z, y = me // NY, me % NY

        def zat(d):
            return lax.rem(z + d + 2 * nz, nz)

        def yat(d):
            return lax.rem(y + d + 2 * NY, NY)

        def zdev(d):
            return (zat(d) * NY + y, ten)

        def ydev(d):
            return (z * NY + yat(d), ten)

        barrier = pltpu.get_barrier_semaphore()

        met = [ydev(d) for d in (1, -1, 2)] + [zdev(d) for d in (1, -1, 2, -2, 3, -3, 4)]
        met += [(me, lax.rem(ten + o, n_tensor)) for o in range(1, n_tensor)]
        if FULL:
            met += [(zat(dz) * NY + yat(dy), ten) for dz in range(1, nz) for dy in range(1, NY)]

        def greet():
            for dev in met:
                pl.semaphore_signal(barrier, inc=1, device_id=dev, device_id_type=MESH)
            pl.semaphore_wait(barrier, len(met))

        own_copies = []
        for k, (c0, w, _) in enumerate(ROUNDS):
            cols = pl.ds(c0, w)
            own_copies.append(
                pltpu.make_async_copy(
                    g_ref.at[:, :, :, :, cols], buf["own"].at[:, :, :, :, cols], own_sem.at[k]
                )
            )
        loads = [
            pltpu.make_async_copy(lr_ref, buf["lroot"], load_sem.at[0]),
            pltpu.make_async_copy(rr_ref, buf["rroot"], load_sem.at[1]),
            pltpu.make_async_copy(lf_ref, buf["lfac"], load_sem.at[2]),
            pltpu.make_async_copy(rf_ref, buf["rfac"], load_sem.at[3]),
        ]
        copies = {}

        def put(name, src, dst, dev):
            i = messages[name]
            copies[name] = pltpu.make_async_remote_copy(
                src_ref=src, dst_ref=dst, send_sem=send.at[i], recv_sem=recv.at[i],
                device_id=dev, device_id_type=MESH,
            )
            copies[name].start()

        def total(parts):
            if len(parts) == 2:
                return parts[0] + parts[1]
            acc = parts[0].astype(F32)
            for p in parts[1:]:
                acc = acc + p.astype(F32)
            return acc.astype(BF16)

        events = []

        def event(name, emit, rank, needs=(), after=(), sends=(), cost=0.2):
            events.append(dict(name=name, emit=emit, rank=rank, needs=needs, after=after, sends=sends, cost=cost))

        loaded = set()

        def need_own(k):
            if k not in loaded:
                loaded.add(k)
                own_copies[k].wait()

        finals = {k: [] for k in range(n_rounds)}
        for i, (k, c0, w, b0, nb, yfirst, s, forms) in enumerate(sets):
            yform, zform = forms if yfirst else forms[::-1]
            cols = pl.ds(c0, w)
            blocks = pl.ds(b0, nb)
            kib = nb * strip * w * 2 / 1024

            def own_y(src, i=i, blocks=blocks, cols=cols, yfirst=yfirst):
                return (lambda d: src.at[blocks, :, yat(d), :, cols]) if yfirst else (lambda d: src.at[:, yat(d)])

            def own_z(src, i=i, blocks=blocks, cols=cols, yfirst=yfirst):
                return (lambda d: src.at[:, zat(d)]) if yfirst else (lambda d: src.at[blocks, zat(d), :, :, cols])

            def fold(dst, parts, lead, n_lead, nb=nb):
                if not lead:
                    for b in range(nb):
                        dst[b] = total([p[b] for p in parts])
                    return

                def one(v, _):
                    for b in range(nb):
                        dst[b, v] = total([p[b, v] for p in parts])
                    return 0

                lax.fori_loop(0, n_lead, one, 0)

            first_y, first_z = yfirst, not yfirst
            ysize = kib * nz if yfirst else kib
            zsize = kib if yfirst else kib * NY
            mid = buf[f"mid_{i}"]
            y_raw = own_y(g_ref if yfirst else mid)
            y_own = own_y(buf["own"] if yfirst else mid)
            z_raw = own_z(mid if yfirst else g_ref)
            z_own = own_z(mid if yfirst else buf["own"])
            agg = buf[f"agg_{k}"].at[blocks]
            ry1, ry2, ry3, sy = (buf.get(f"{n}_{i}") for n in ("ry1", "ry2", "ry3", "sy"))
            rza, rzb, sza, szb = (buf.get(f"{n}_{i}") for n in ("rza", "rzb", "sza", "szb"))
            ry, rz = buf.get(f"ry_{i}"), buf.get(f"rz_{i}")
            ylead = (yfirst, nz)
            zlead = (not yfirst, NY)
            up, down = s, -s
            yl, zl = {1: f"y{s}", -1: f"y{-s}"}, {1: f"z{s}", -1: f"z{-s}"}
            yk = k * 10 + (0 if yfirst else 5)
            zk = k * 10 + (5 if yfirst else 0)
            ybase = () if yfirst else (f"zdone_{i}",)
            zbase = (f"ydone_{i}",) if yfirst else ()

            def y0(i=i, y_raw=y_raw, ry1=ry1, ry3=ry3, s=s):
                put(f"y1_{i}", y_raw(2 * s), ry1, ydev(s))
                put(f"y3_{i}", y_raw(-s), ry3, ydev(-s))

            def y1(i=i, k=k, y_own=y_own, ry1=ry1, ry2=ry2, sy=sy, s=s, fold=fold, ylead=ylead):
                need_own(k)
                copies[f"y1_{i}"].wait_recv()
                fold(sy, [ry1, y_own(s)], *ylead)
                put(f"y2_{i}", sy, ry2, ydev(s))

            def y2(i=i, k=k, y_own=y_own, ry2=ry2, ry3=ry3, fold=fold, ylead=ylead,
                   dst=mid if yfirst else agg):
                need_own(k)
                copies[f"y2_{i}"].wait_recv()
                copies[f"y3_{i}"].wait_recv()
                fold(dst, [ry2, ry3, y_own(0)], *ylead)

            def straight(name, raw, into, far, dev):
                i = messages[name]
                for at, d in enumerate(far):
                    pltpu.make_async_remote_copy(
                        src_ref=raw(d), dst_ref=into.at[at], send_sem=send.at[i], recv_sem=recv.at[i],
                        device_id=dev(d), device_id_type=MESH,
                    ).start()
                copies[name] = Whole(into, send.at[i], recv.at[i])

            def ystart(i=i, y_raw=y_raw, ry=ry, straight=straight):
                straight(f"y_{i}", y_raw, ry, YFAR, ydev)

            def yend(i=i, k=k, y_own=y_own, ry=ry, fold=fold, ylead=ylead, dst=mid if yfirst else agg):
                need_own(k)
                copies[f"y_{i}"].wait_recv()
                fold(dst, [y_own(0)] + [ry.at[at] for at in range(NY - 1)], *ylead)

            def zflood(i=i, z_raw=z_raw, rz=rz, straight=straight):
                straight(f"z_{i}", z_raw, rz, ZFAR, zdev)

            def zsink(i=i, k=k, z_own=z_own, rz=rz, fold=fold, zlead=zlead, dst=agg if yfirst else mid):
                need_own(k)
                copies[f"z_{i}"].wait_recv()
                fold(dst, [z_own(0)] + [rz.at[at] for at in range(nz - 1)], *zlead)

            if yform == "c":
                event(f"y0_{i}", y0, yk, after=ybase,
                      sends=[(f"y1_{i}", yl[1], ysize), (f"y3_{i}", yl[-1], ysize)])
                event(f"y1_{i}", y1, yk - 1, needs=[f"y1_{i}"], sends=[(f"y2_{i}", yl[1], ysize)], cost=0.1 + FOLD * ysize * 2)
                event(f"ydone_{i}", y2, yk - 2, needs=[f"y2_{i}", f"y3_{i}"], cost=0.1 + FOLD * ysize * 3)
            else:
                event(f"y0_{i}", ystart, yk, after=ybase,
                      sends=[(f"y+_{i}", yl[1], 2 * ysize), (f"y-_{i}", yl[-1], 2 * ysize)])
                event(f"ydone_{i}", yend, yk - 2, needs=[f"y+_{i}", f"y-_{i}"], cost=0.1 + FOLD * ysize * 4)
            if zform == "d":
                event(f"z0_{i}", zflood, zk, after=zbase,
                      sends=[(f"z+_{i}", zl[1], 8 * zsize), (f"z-_{i}", zl[-1], 8 * zsize)])
                event(f"zdone_{i}", zsink, zk - 2, needs=[f"z+_{i}", f"z-_{i}"], cost=0.1 + FOLD * zsize * 8)

            def zstart(i=i, z_raw=z_raw, rza=rza, rzb=rzb, s=s):
                put(f"a0_{i}", z_raw(half * s), rza.at[0], zdev(s))
                put(f"b0_{i}", z_raw(-(half - 1) * s), rzb.at[0], zdev(-s))

            if zform == "c":
                event(f"z0_{i}", zstart, zk, after=zbase,
                      sends=[(f"a0_{i}", zl[1], zsize), (f"b0_{i}", zl[-1], zsize)])
                for h in range(1, half):
                    def za(i=i, k=k, h=h, z_own=z_own, rza=rza, sza=sza, s=s, fold=fold, zlead=zlead):
                        need_own(k)
                        copies[f"a{h - 1}_{i}"].wait_recv()
                        fold(sza.at[h - 1], [rza.at[h - 1], z_own((half - h) * s)], *zlead)
                        put(f"a{h}_{i}", sza.at[h - 1], rza.at[h], zdev(s))

                    event(f"za{h}_{i}", za, zk - 1, needs=[f"a{h - 1}_{i}"], sends=[(f"a{h}_{i}", zl[1], zsize)],
                          cost=0.1 + FOLD * zsize * 2)
                for h in range(1, half - 1):
                    def zb(i=i, k=k, h=h, z_own=z_own, rzb=rzb, szb=szb, s=s, fold=fold, zlead=zlead):
                        need_own(k)
                        copies[f"b{h - 1}_{i}"].wait_recv()
                        fold(szb.at[h - 1], [rzb.at[h - 1], z_own(-(half - 1 - h) * s)], *zlead)
                        put(f"b{h}_{i}", szb.at[h - 1], rzb.at[h], zdev(-s))

                    event(f"zb{h}_{i}", zb, zk - 1, needs=[f"b{h - 1}_{i}"], sends=[(f"b{h}_{i}", zl[-1], zsize)],
                          cost=0.1 + FOLD * zsize * 2)

                def zend(i=i, k=k, z_own=z_own, rza=rza, rzb=rzb, fold=fold, zlead=zlead,
                         dst=agg if yfirst else mid):
                    need_own(k)
                    copies[f"a{half - 1}_{i}"].wait_recv()
                    copies[f"b{half - 2}_{i}"].wait_recv()
                    fold(dst, [rza.at[half - 1], rzb.at[half - 2], z_own(0)], *zlead)

                event(f"zdone_{i}", zend, zk - 2, needs=[f"a{half - 1}_{i}", f"b{half - 2}_{i}"],
                      cost=0.1 + FOLD * zsize * 3)
            finals[k].append(f"zdone_{i}" if yfirst else f"ydone_{i}")

        def block_of(device):
            found = jnp.int32(0)
            for j in range(nb_all):
                found = jnp.where(owners_ref[0, j] == device, j, found)
            return found

        def peer(o):
            dz, dy = o // NY, o % NY
            step = jnp.where(dz % 2 == 1, (dz + 1) // 2, nz - dz // 2)
            return lax.rem(z + step, nz) * NY + lax.rem(y + dy, NY)

        for k, (c0, w, _) in enumerate(ROUNDS):
            kib = strip * w * 2 / 1024

            def route(k=k):
                agg, stage, grad = (buf[f"{n}_{k}"] for n in ("agg", "stage", "grad"))

                def one(o, _):
                    to = peer(o)
                    stage[o] = agg[block_of(to)]
                    pltpu.make_async_remote_copy(
                        src_ref=stage.at[o], dst_ref=grad.at[me], send_sem=a2a_send.at[k], recv_sem=a2a_recv.at[k],
                        device_id=(to, ten), device_id_type=MESH,
                    ).start()
                    return 0

                lax.fori_loop(1, n_dp, one, 0)
                grad[me] = agg[block_of(me)]

            event(f"route_{k}", route, k * 10 - 3, after=finals[k],
                  sends=[(f"rz{q}_{k}", f"z{q}", kib * 8 * NY) for q in (1, -1)]
                  + [(f"ry{q}_{k}", f"y{q}", kib * 2 * nz) for q in (1, -1)], cost=1.0)

        def a2a_all(sem, ref):
            part = ref.at[pl.ds(0, n_dp - 1)]
            return pltpu.make_async_copy(part, part, sem)

        waited = []

        def land(k):
            a2a_all(a2a_recv.at[k], buf[f"grad_{k}"]).wait()
            if not waited:
                waited.append(k)
                for c in loads:
                    c.wait()
            w = ROUNDS[k][1]
            gk = buf[f"grad_{k}"][...].reshape(width, w)
            buf["half"][:, ROUNDS[k][0]:ROUNDS[k][0] + w] = jnp.dot(
                buf["lroot"][...], gk, preferred_element_type=F32).astype(BF16)
            gf = gk.astype(F32)
            folded = jnp.sum((gf * gf).reshape(width // 8, 8, w), axis=0)
            buf["gsq"][k] = sum(folded[:, c:c + 128] for c in range(0, w, 128))

        for k in range(n_rounds):
            event(f"land_{k}", functools.partial(land, k), k * 10 - 4,
                  needs=[f"rz{q}_{k}" for q in (1, -1)] + [f"ry{q}_{k}" for q in (1, -1)], cost=0.7)

        for c in own_copies:
            c.start()
        greet()
        order, _ = plan(events, *MODEL)
        started = False
        for e in order:
            if not started and (e["needs"] or e is order[-1]):
                started = True
                for c in loads:
                    c.start()
            e["emit"]()


        def whole():
            parts = [buf[f"grad_{k}"][...].reshape(width, ROUNDS[k][1]) for k in range(n_rounds)]
            return parts[0] if len(parts) == 1 else jnp.concatenate(parts, axis=1)

        owned = jnp.int32(0)
        for j in range(nb_all):
            owned = owned + jnp.where(owners_ref[0, j] == me, 1, 0)
        mine = owned > 0
        tall = 128
        pre = buf["pre"]
        squares = jnp.zeros((8, width), F32)
        for i in range(width // tall):
            rows = pl.ds(i * tall, tall)
            p = jnp.dot(buf["half"][rows, :], buf["rroot"][...], preferred_element_type=F32)
            pre[rows, :] = p
            squares = squares + jnp.sum((p * p).reshape(tall // 8, 8, width), axis=0)
        grad_squares = jnp.sum(buf["gsq"][...], axis=0)
        count = width * width
        grad_mean = jnp.sum(grad_squares, axis=(0, 1), keepdims=True) / count
        pre_mean = jnp.sum(squares, axis=(0, 1), keepdims=True) / count
        factor = jnp.sqrt(grad_mean + epsilon) / jnp.sqrt(pre_mean + epsilon)
        for i in range(width // tall):
            rows = pl.ds(i * tall, tall)
            per = tall // strip
            shaped = (pre[rows, :] * factor).astype(BF16)
            buf["shaped"][pl.ds(i * per, per)] = shaped.reshape(per, strip, width)

        shaped, arrived = buf["shaped"], buf["arrived"]

        def give(o, _):
            to = peer(o)
            pltpu.make_async_remote_copy(
                src_ref=shaped.at[to], dst_ref=arrived.at[me], send_sem=a2a_send.at[n_rounds],
                recv_sem=a2a_recv.at[n_rounds], device_id=(to, ten), device_id_type=MESH,
            ).start()
            return 0

        local = (pre_mean / (pre_mean + epsilon)) * (grad_mean + epsilon) * count
        local = lax.select(mine, local, jnp.zeros_like(local))
        local = jnp.broadcast_to(local, (8, 128))

        def exchange(ref, n, dev, at, value):
            ref[0] = value
            if n == 1:
                return value
            for o in range(1, n):
                pltpu.make_async_remote_copy(
                    src_ref=ref.at[0], dst_ref=ref.at[o], send_sem=sum_send.at[at], recv_sem=sum_recv.at[at],
                    device_id=dev(o), device_id_type=MESH,
                ).start()

            def finish():
                part = ref.at[pl.ds(1, n - 1)]
                pltpu.make_async_copy(part, part, sum_recv.at[at]).wait()
                return jnp.sum(ref[...], axis=0)

            return finish

        finish = exchange(buf["sum_t"], n_tensor, lambda o: (me, lax.rem(ten + o, n_tensor)), 0, local)
        lax.fori_loop(1, n_dp, give, 0)
        arrived[me] = shaped[me]

        gram_weight = (1.0 - decay_rate) / width

        def statistic(factor_ref, gram):
            add = gram_weight * gram
            add = lax.select(mine, add, jnp.zeros_like(add))
            return decay_rate * factor_ref + add

        for i in range(width // tall):
            rows = pl.ds(i * tall, tall)
            gram = jnp.zeros((tall, width), F32)
            for k in range(n_rounds):
                gk = buf[f"grad_{k}"]
                per = tall // strip
                top = gk[pl.ds(i * per, per)].reshape(tall, ROUNDS[k][1])
                gram = gram + lax.dot_general(top, gk[...].reshape(width, ROUNDS[k][1]), (((1,), (1,)), ((), ())),
                                              preferred_element_type=F32)
            nl_ref[rows, :] = statistic(buf["lfac"][rows, :], gram)
        if n_tensor > 1:
            local = finish()
        finish = exchange(buf["sum_y"], NY, lambda o: (z * NY + lax.rem(y + o, NY), ten), 1, local)
        grad = whole()
        flipped = grad.T
        for i in range(width // tall):
            rows = pl.ds(i * tall, tall)
            gram = jnp.dot(flipped[i * tall:(i + 1) * tall], grad, preferred_element_type=F32)
            nr_ref[rows, :] = statistic(buf["rfac"][rows, :], gram)
        local = finish()
        finish = exchange(buf["sum_z"], nz, lambda o: (lax.rem(z + o, nz) * NY + y, ten), 2, local)
        local = finish()
        entries = nb_all * n_tensor * width * width
        scale = 1.0 / jnp.sqrt(local / entries + epsilon)
        scale = jnp.broadcast_to(scale[0:1, 0:1], (strip, width))
        a2a_all(a2a_recv.at[n_rounds], arrived).wait()
        for j in range(nb_all):
            dir_ref[j] = (arrived[owners_ref[0, j]].astype(F32) * scale).astype(BF16)

        for c in copies.values():
            c.wait_send()
        for k in range(n_rounds):
            a2a_all(a2a_send.at[k], buf[f"stage_{k}"]).wait()
        a2a_all(a2a_send.at[n_rounds], shaped).wait()
        for at, (n, ref) in enumerate(((n_tensor, buf["sum_t"]), (NY, buf["sum_y"]), (nz, buf["sum_z"]))):
            if n > 1:
                part = ref.at[pl.ds(1, n - 1)]
                pltpu.make_async_copy(part, part, sum_send.at[at]).wait()

    hbm = pl.BlockSpec(memory_space=pl.ANY)
    vmem = pl.BlockSpec(memory_space=pltpu.VMEM)
    new_left, new_right, directions = pl.pallas_call(
        kernel,
        out_shape=(
            pltpu.VMEM((width, width), F32),
            pltpu.VMEM((width, width), F32),
            pltpu.VMEM((nb_all, strip, width), BF16),
        ),
        in_specs=[pl.BlockSpec(memory_space=pltpu.SMEM)] + [hbm] * 5,
        out_specs=(vmem, vmem, vmem),
        scratch_shapes=shapes
        + [
            pltpu.SemaphoreType.DMA((n_msg,)),
            pltpu.SemaphoreType.DMA((n_msg,)),
            pltpu.SemaphoreType.DMA((n_rounds,)),
            pltpu.SemaphoreType.DMA((4,)),
            pltpu.SemaphoreType.DMA((n_rounds + 1,)),
            pltpu.SemaphoreType.DMA((n_rounds + 1,)),
            pltpu.SemaphoreType.DMA((3,)),
            pltpu.SemaphoreType.DMA((3,)),
        ],
        compiler_params=pltpu.CompilerParams(
            collective_id=0, has_side_effects=True, vmem_limit_bytes=58 * 1024 * 1024
        ),
        name="shampoo",
    )(owners, g, left_factor[0, 0], right_factor[0, 0], left_root[0, 0], right_root[0, 0])
    return new_left[None, None], new_right[None, None], directions


def solution(mesh):
    nz = mesh.shape["dp"] // NY
    return jax.shard_map(
        functools.partial(per_device, nz, mesh.shape["tensor"]),
        mesh=mesh,
        in_specs=(
            P("dp", "tensor", None, None),
            P("tensor", None),
            P("tensor", "dp", None, None),
            P("tensor", "dp", None, None),
            P("tensor", "dp", None, None),
            P("tensor", "dp", None, None),
        ),
        out_specs=(
            P("tensor", "dp", None, None),
            P("tensor", "dp", None, None),
            P("tensor", "dp", None),
        ),
        check_vma=False,
    )
```

```python
import functools

import jax
import jax.numpy as jnp
from jax import lax
from jax.experimental import pallas as pl
from jax.experimental.pallas import tpu as pltpu
from jax.sharding import PartitionSpec as P

MESH = pl.DeviceIdType.MESH
F32 = jnp.float32
BF16 = jnp.bfloat16
decay_rate = 0.95
epsilon = 1e-06
NY = 4

ROUNDS = (
    (0, 128, (
        (4, "y", 1, "ct", 13.1),
        (3, "y", -1, "cc", 6.5),
        (1, "z", 1, "cd", 7.2),
    )),
    (128, 256, (
        (2, "y", -1, "ct", 15.8),
        (3, "z", 1, "cd", 12.0),
        (2, "z", -1, "cd", 21.6),
        (1, "y", 1, "cd", 16.8),
    )),
    (384, 128, (
        (4, "y", -1, "cd", 29.3),
        (3, "z", 1, "cd", 19.8),
        (1, "y", 1, "cd", 21.2),
    )),
)
FULL = False
GIVE = "near"
FIRST = ((4, 12), (20, 28))
LAST = ((1, 4), (12, 20), (28, 32))
FOLD = 0.002
YFAR = (1, -1, 2)
ZFAR = (1, -1, 2, -2, 3, -3, 4)
MODEL = (46.5, 2.2, 3.0)


class Whole:
    def __init__(self, ref, send, recv):
        self.ref, self.send, self.recv = ref, send, recv

    def wait_recv(self):
        pltpu.make_async_copy(self.ref, self.ref, self.recv).wait()

    def wait_send(self):
        pltpu.make_async_copy(self.ref, self.ref, self.send).wait()


def plan(events, rate, latency, lead):
    free = dict.fromkeys(("y1", "y-1", "z1", "z-1"), 0.0)
    arrive, done, order, now = {}, {}, [], 0.0
    left = list(events)
    while left:
        best = None
        for e in left:
            if any(m not in arrive for m in e["needs"]) or any(d not in done for d in e["after"]):
                continue
            ready = max([arrive[m] for m in e["needs"]] + [now])
            if not e["needs"] and not e["after"]:
                ready = max([now] + [free[link] - lead for _, link, _ in e["sends"]])
            key = (ready, e["rank"])
            if best is None or key < best[0]:
                best = (key, e)
        (ready, _), e = best
        now = ready + e["cost"]
        for name, link, kib in e["sends"]:
            free[link] = max(free[link], now) + kib * 1.024 / rate
            arrive[name] = free[link] + latency
        done[e["name"]] = now
        order.append(e)
        left.remove(e)
    return order, now


def per_device(nz, n_tensor, gradients, owners, left_factor, right_factor, left_root, right_root):
    nb_all, width = gradients.shape[1], gradients.shape[2]
    n_dp = nz * NY
    strip = width // n_dp
    g = gradients.reshape(nb_all, nz, NY, strip, width)
    sets = []
    for k, (c0, w, found) in enumerate(ROUNDS):
        b0 = 0
        for nb, axis, s, forms, rank in found:
            sets.append((k, c0, w, b0, nb, axis == "y", s, (forms, rank)))
            b0 += nb
    names, shapes = [], []

    def buffer(name, shape, dtype=BF16):
        names.append(name)
        shapes.append(pltpu.VMEM(shape, dtype))

    messages = {}
    half = nz // 2
    for i, (k, c0, w, b0, nb, yfirst, s, forms) in enumerate(sets):
        ychunk = (nb, nz, strip, w) if yfirst else (nb, strip, w)
        zchunk = (nb, strip, w) if yfirst else (nb, NY, strip, w)
        forms = forms[0]
        yform, zform = forms if yfirst else forms[::-1]
        buffer(f"mid_{i}", ychunk if yfirst else zchunk)
        if yform == "c":
            for n in ("ry1", "ry2", "ry3", "sy"):
                buffer(f"{n}_{i}", ychunk)
            found = ["y1", "y2", "y3"]
        else:
            buffer(f"ry_{i}", (NY - 1,) + ychunk)
            found = ["y"]
        if zform == "c":
            buffer(f"rza_{i}", (half,) + zchunk)
            buffer(f"rzb_{i}", (half - 1,) + zchunk)
            buffer(f"sza_{i}", (half - 1,) + zchunk)
            buffer(f"szb_{i}", (half - 2,) + zchunk)
            found += [f"a{h}" for h in range(half)] + [f"b{h}" for h in range(half - 1)]
        elif zform == "t":
            buffer(f"rt_{i}", (7,) + zchunk)
            buffer(f"st_{i}", (2,) + zchunk)
            found += [f"t{h}" for h in range(7)]
        else:
            buffer(f"rz_{i}", (nz - 1,) + zchunk)
            found += ["z"]
        for n in found:
            messages[f"{n}_{i}"] = len(messages)
    for k, (c0, w, _) in enumerate(ROUNDS):
        buffer(f"agg_{k}", (nb_all, strip, w))
        buffer(f"stage_{k}", (n_dp, strip, w))
        buffer(f"grad_{k}", (n_dp, strip, w))
    buffer("own", (nb_all, nz, NY, strip, width))
    buffer("lroot", (width, width))
    buffer("rroot", (width, width))
    buffer("lfac", (width, width), F32)
    buffer("rfac", (width, width), F32)
    buffer("pre", (n_dp, strip, width))
    buffer("half", (width, width))
    buffer("gsq", (len(ROUNDS), 8, 128), F32)
    buffer("arrived", (n_dp, strip, width))
    buffer("sum_t", (n_tensor, 8, 128), F32)
    buffer("sum_y", (NY, 8, 128), F32)
    buffer("sum_z", (nz, 8, 128), F32)

    n_msg = len(messages)
    n_rounds = len(ROUNDS)

    def kernel(owners_ref, g_ref, lf_ref, rf_ref, lr_ref, rr_ref, nl_ref, nr_ref, dir_ref, *scratch):
        buf = dict(zip(names, scratch))
        send, recv, own_sem, load_sem, a2a_send, a2a_recv, sum_send, sum_recv = scratch[len(names):]
        me, ten = lax.axis_index("dp"), lax.axis_index("tensor")
        z, y = me // NY, me % NY

        def zat(d):
            return lax.rem(z + d + 2 * nz, nz)

        def yat(d):
            return lax.rem(y + d + 2 * NY, NY)

        def zdev(d):
            return (zat(d) * NY + y, ten)

        def ydev(d):
            return (z * NY + yat(d), ten)

        barrier = pltpu.get_barrier_semaphore()

        met = [ydev(d) for d in (1, -1, 2)] + [zdev(d) for d in (1, -1, 2, -2, 3, -3, 4)]
        met += [(me, lax.rem(ten + o, n_tensor)) for o in range(1, n_tensor)]
        if FULL:
            met += [(zat(dz) * NY + yat(dy), ten) for dz in range(1, nz) for dy in range(1, NY)]

        def greet():
            for dev in met:
                pl.semaphore_signal(barrier, inc=1, device_id=dev, device_id_type=MESH)
            pl.semaphore_wait(barrier, len(met))

        own_copies = []
        for k, (c0, w, _) in enumerate(ROUNDS):
            cols = pl.ds(c0, w)
            own_copies.append(
                pltpu.make_async_copy(
                    g_ref.at[:, :, :, :, cols], buf["own"].at[:, :, :, :, cols], own_sem.at[k]
                )
            )
        loads = [
            pltpu.make_async_copy(lr_ref, buf["lroot"], load_sem.at[0]),
            pltpu.make_async_copy(rr_ref, buf["rroot"], load_sem.at[1]),
            pltpu.make_async_copy(lf_ref, buf["lfac"], load_sem.at[2]),
            pltpu.make_async_copy(rf_ref, buf["rfac"], load_sem.at[3]),
        ]
        copies = {}

        def put(name, src, dst, dev):
            i = messages[name]
            copies[name] = pltpu.make_async_remote_copy(
                src_ref=src, dst_ref=dst, send_sem=send.at[i], recv_sem=recv.at[i],
                device_id=dev, device_id_type=MESH,
            )
            copies[name].start()

        def total(parts):
            if len(parts) == 2:
                return parts[0] + parts[1]
            acc = parts[0].astype(F32)
            for p in parts[1:]:
                acc = acc + p.astype(F32)
            return acc.astype(BF16)

        events = []

        def event(name, emit, rank, needs=(), after=(), sends=(), cost=0.2):
            events.append(dict(name=name, emit=emit, rank=rank, needs=needs, after=after, sends=sends, cost=cost))

        loaded = set()

        def need_own(k):
            if k not in loaded:
                loaded.add(k)
                own_copies[k].wait()

        finals = {k: [] for k in range(n_rounds)}
        for i, (k, c0, w, b0, nb, yfirst, s, forms) in enumerate(sets):
            forms, rank = forms
            yform, zform = forms if yfirst else forms[::-1]
            cols = pl.ds(c0, w)
            blocks = pl.ds(b0, nb)
            kib = nb * strip * w * 2 / 1024

            def own_y(src, i=i, blocks=blocks, cols=cols, yfirst=yfirst):
                return (lambda d: src.at[blocks, :, yat(d), :, cols]) if yfirst else (lambda d: src.at[:, yat(d)])

            def own_z(src, i=i, blocks=blocks, cols=cols, yfirst=yfirst):
                return (lambda d: src.at[:, zat(d)]) if yfirst else (lambda d: src.at[blocks, zat(d), :, :, cols])

            def fold(dst, parts, lead, n_lead, nb=nb):
                if not lead:
                    for b in range(nb):
                        dst[b] = total([p[b] for p in parts])
                    return

                def one(v, _):
                    for b in range(nb):
                        dst[b, v] = total([p[b, v] for p in parts])
                    return 0

                lax.fori_loop(0, n_lead, one, 0)

            first_y, first_z = yfirst, not yfirst
            ysize = kib * nz if yfirst else kib
            zsize = kib if yfirst else kib * NY
            mid = buf[f"mid_{i}"]
            y_raw = own_y(g_ref if yfirst else mid)
            y_own = own_y(buf["own"] if yfirst else mid)
            z_raw = own_z(mid if yfirst else g_ref)
            z_own = own_z(mid if yfirst else buf["own"])
            agg = buf[f"agg_{k}"].at[blocks]
            ry1, ry2, ry3, sy = (buf.get(f"{n}_{i}") for n in ("ry1", "ry2", "ry3", "sy"))
            rza, rzb, sza, szb = (buf.get(f"{n}_{i}") for n in ("rza", "rzb", "sza", "szb"))
            ry, rz = buf.get(f"ry_{i}"), buf.get(f"rz_{i}")
            rt, st = buf.get(f"rt_{i}"), buf.get(f"st_{i}")
            ylead = (yfirst, nz)
            zlead = (not yfirst, NY)
            up, down = s, -s
            yl, zl = {1: f"y{s}", -1: f"y{-s}"}, {1: f"z{s}", -1: f"z{-s}"}
            yk, zk = (rank, k * 10 + 5) if yfirst else (k * 10 + 5, rank)
            yr, zr = (k * 10, zk) if yfirst else (yk, k * 10)
            ybase = () if yfirst else (f"zdone_{i}",)
            zbase = (f"ydone_{i}",) if yfirst else ()

            def y0(i=i, y_raw=y_raw, ry1=ry1, ry3=ry3, s=s):
                put(f"y1_{i}", y_raw(2 * s), ry1, ydev(s))
                put(f"y3_{i}", y_raw(-s), ry3, ydev(-s))

            def y1(i=i, k=k, y_own=y_own, ry1=ry1, ry2=ry2, sy=sy, s=s, fold=fold, ylead=ylead):
                need_own(k)
                copies[f"y1_{i}"].wait_recv()
                fold(sy, [ry1, y_own(s)], *ylead)
                put(f"y2_{i}", sy, ry2, ydev(s))

            def y2(i=i, k=k, y_own=y_own, ry2=ry2, ry3=ry3, fold=fold, ylead=ylead,
                   dst=mid if yfirst else agg):
                need_own(k)
                copies[f"y2_{i}"].wait_recv()
                copies[f"y3_{i}"].wait_recv()
                fold(dst, [ry2, ry3, y_own(0)], *ylead)

            def straight(name, raw, into, far, dev):
                i = messages[name]
                for at, d in enumerate(far):
                    pltpu.make_async_remote_copy(
                        src_ref=raw(d), dst_ref=into.at[at], send_sem=send.at[i], recv_sem=recv.at[i],
                        device_id=dev(d), device_id_type=MESH,
                    ).start()
                copies[name] = Whole(into, send.at[i], recv.at[i])

            def ystart(i=i, y_raw=y_raw, ry=ry, straight=straight):
                straight(f"y_{i}", y_raw, ry, YFAR, ydev)

            def yend(i=i, k=k, y_own=y_own, ry=ry, fold=fold, ylead=ylead, dst=mid if yfirst else agg):
                need_own(k)
                copies[f"y_{i}"].wait_recv()
                fold(dst, [y_own(0)] + [ry.at[at] for at in range(NY - 1)], *ylead)

            def zflood(i=i, z_raw=z_raw, rz=rz, straight=straight):
                straight(f"z_{i}", z_raw, rz, ZFAR, zdev)

            def zsink(i=i, k=k, z_own=z_own, rz=rz, fold=fold, zlead=zlead, dst=agg if yfirst else mid):
                need_own(k)
                copies[f"z_{i}"].wait_recv()
                fold(dst, [z_own(0)] + [rz.at[at] for at in range(nz - 1)], *zlead)

            def zpairs(i=i, z_raw=z_raw, rt=rt, s=s):
                for at, (chunk, to) in enumerate(((4, 2), (3, 1), (-3, -1), (1, 1), (-1, -1))):
                    put(f"t{at}_{i}", z_raw(chunk * s), rt.at[at], zdev(to * s))

            def zjoin(i=i, k=k, z_own=z_own, rt=rt, st=st, s=s, fold=fold, zlead=zlead):
                need_own(k)
                for at in range(3):
                    copies[f"t{at}_{i}"].wait_recv()
                fold(st.at[0], [rt.at[0], rt.at[1], z_own(2 * s)], *zlead)
                put(f"t5_{i}", st.at[0], rt.at[5], zdev(2 * s))
                fold(st.at[1], [rt.at[2], z_own(-2 * s)], *zlead)
                put(f"t6_{i}", st.at[1], rt.at[6], zdev(-2 * s))

            def zmeet(i=i, k=k, z_own=z_own, rt=rt, fold=fold, zlead=zlead, dst=agg if yfirst else mid):
                need_own(k)
                for at in range(3, 7):
                    copies[f"t{at}_{i}"].wait_recv()
                fold(dst, [z_own(0)] + [rt.at[at] for at in range(3, 7)], *zlead)

            if yform == "c":
                event(f"y0_{i}", y0, yk, after=ybase,
                      sends=[(f"y1_{i}", yl[1], ysize), (f"y3_{i}", yl[-1], ysize)])
                event(f"y1_{i}", y1, yr - 1, needs=[f"y1_{i}"], sends=[(f"y2_{i}", yl[1], ysize)], cost=0.1 + FOLD * ysize * 2)
                event(f"ydone_{i}", y2, yr - 2, needs=[f"y2_{i}", f"y3_{i}"], cost=0.1 + FOLD * ysize * 3)
            else:
                event(f"y0_{i}", ystart, yk, after=ybase,
                      sends=[(f"y+_{i}", yl[1], 2 * ysize), (f"y-_{i}", yl[-1], 2 * ysize)])
                event(f"ydone_{i}", yend, yr - 2, needs=[f"y+_{i}", f"y-_{i}"], cost=0.1 + FOLD * ysize * 4)
            if zform == "t":
                event(f"z0_{i}", zpairs, zk, after=zbase,
                      sends=[(f"t+_{i}", zl[1], 3 * zsize), (f"t-_{i}", zl[-1], zsize),
                             (f"T+_{i}", zl[1], zsize), (f"T-_{i}", zl[-1], zsize)])
                event(f"z1_{i}", zjoin, zr - 1, needs=[f"t+_{i}", f"t-_{i}"],
                      sends=[(f"u+_{i}", zl[1], 2 * zsize), (f"u-_{i}", zl[-1], 2 * zsize)], cost=0.2 + FOLD * zsize * 5)
                event(f"zdone_{i}", zmeet, zr - 2, needs=[f"u+_{i}", f"u-_{i}", f"T+_{i}", f"T-_{i}"],
                      cost=0.1 + FOLD * zsize * 5)
            if zform == "d":
                event(f"z0_{i}", zflood, zk, after=zbase,
                      sends=[(f"z+_{i}", zl[1], 8 * zsize), (f"z-_{i}", zl[-1], 8 * zsize)])
                event(f"zdone_{i}", zsink, zr - 2, needs=[f"z+_{i}", f"z-_{i}"], cost=0.1 + FOLD * zsize * 8)

            def zstart(i=i, z_raw=z_raw, rza=rza, rzb=rzb, s=s):
                put(f"a0_{i}", z_raw(half * s), rza.at[0], zdev(s))
                put(f"b0_{i}", z_raw(-(half - 1) * s), rzb.at[0], zdev(-s))

            if zform == "c":
                event(f"z0_{i}", zstart, zk, after=zbase,
                      sends=[(f"a0_{i}", zl[1], zsize), (f"b0_{i}", zl[-1], zsize)])
                for h in range(1, half):
                    def za(i=i, k=k, h=h, z_own=z_own, rza=rza, sza=sza, s=s, fold=fold, zlead=zlead):
                        need_own(k)
                        copies[f"a{h - 1}_{i}"].wait_recv()
                        fold(sza.at[h - 1], [rza.at[h - 1], z_own((half - h) * s)], *zlead)
                        put(f"a{h}_{i}", sza.at[h - 1], rza.at[h], zdev(s))

                    event(f"za{h}_{i}", za, zr - 1, needs=[f"a{h - 1}_{i}"], sends=[(f"a{h}_{i}", zl[1], zsize)],
                          cost=0.1 + FOLD * zsize * 2)
                for h in range(1, half - 1):
                    def zb(i=i, k=k, h=h, z_own=z_own, rzb=rzb, szb=szb, s=s, fold=fold, zlead=zlead):
                        need_own(k)
                        copies[f"b{h - 1}_{i}"].wait_recv()
                        fold(szb.at[h - 1], [rzb.at[h - 1], z_own(-(half - 1 - h) * s)], *zlead)
                        put(f"b{h}_{i}", szb.at[h - 1], rzb.at[h], zdev(-s))

                    event(f"zb{h}_{i}", zb, zr - 1, needs=[f"b{h - 1}_{i}"], sends=[(f"b{h}_{i}", zl[-1], zsize)],
                          cost=0.1 + FOLD * zsize * 2)

                def zend(i=i, k=k, z_own=z_own, rza=rza, rzb=rzb, fold=fold, zlead=zlead,
                         dst=agg if yfirst else mid):
                    need_own(k)
                    copies[f"a{half - 1}_{i}"].wait_recv()
                    copies[f"b{half - 2}_{i}"].wait_recv()
                    fold(dst, [rza.at[half - 1], rzb.at[half - 2], z_own(0)], *zlead)

                event(f"zdone_{i}", zend, zr - 2, needs=[f"a{half - 1}_{i}", f"b{half - 2}_{i}"],
                      cost=0.1 + FOLD * zsize * 3)
            finals[k].append(f"zdone_{i}" if yfirst else f"ydone_{i}")

        def block_of(device):
            found = jnp.int32(0)
            for j in range(nb_all):
                found = jnp.where(owners_ref[0, j] == device, j, found)
            return found

        def peer(o):
            dz, dy = o // NY, o % NY
            step = jnp.where(dz % 2 == 1, (dz + 1) // 2, nz - dz // 2)
            return lax.rem(z + step, nz) * NY + lax.rem(y + dy, NY)

        for k, (c0, w, _) in enumerate(ROUNDS):
            kib = strip * w * 2 / 1024

            def route(k=k):
                agg, stage, grad = (buf[f"{n}_{k}"] for n in ("agg", "stage", "grad"))

                def one(o, _):
                    to = peer(o)
                    stage[o] = agg[block_of(to)]
                    pltpu.make_async_remote_copy(
                        src_ref=stage.at[o], dst_ref=grad.at[me], send_sem=a2a_send.at[k], recv_sem=a2a_recv.at[k],
                        device_id=(to, ten), device_id_type=MESH,
                    ).start()
                    return 0

                lax.fori_loop(1, n_dp, one, 0)
                grad[me] = agg[block_of(me)]

            event(f"route_{k}", route, k * 10 - 3, after=finals[k],
                  sends=[(f"rz{q}_{k}", f"z{q}", kib * 8 * NY) for q in (1, -1)]
                  + [(f"ry{q}_{k}", f"y{q}", kib * 2 * nz) for q in (1, -1)], cost=1.7)

        def a2a_all(sem, ref):
            part = ref.at[pl.ds(0, n_dp - 1)]
            return pltpu.make_async_copy(part, part, sem)

        waited = []

        def land(k):
            a2a_all(a2a_recv.at[k], buf[f"grad_{k}"]).wait()
            if not waited:
                waited.append(k)
                for c in loads:
                    c.wait()
            w = ROUNDS[k][1]
            gk = buf[f"grad_{k}"][...].reshape(width, w)
            buf["half"][:, ROUNDS[k][0]:ROUNDS[k][0] + w] = jnp.dot(
                buf["lroot"][...], gk, preferred_element_type=F32).astype(BF16)
            gf = gk.astype(F32)
            folded = jnp.sum((gf * gf).reshape(width // 8, 8, w), axis=0)
            buf["gsq"][k] = sum(folded[:, c:c + 128] for c in range(0, w, 128))

        for k in range(n_rounds):
            event(f"land_{k}", functools.partial(land, k), k * 10 - 4,
                  needs=[f"rz{q}_{k}" for q in (1, -1)] + [f"ry{q}_{k}" for q in (1, -1)], cost=0.7)

        for c in own_copies:
            c.start()
        greet()
        order, _ = plan(events, *MODEL)
        started = False
        for e in order:
            if not started and (e["needs"] or e is order[-1]):
                started = True
                for c in loads:
                    c.start()
            e["emit"]()


        def whole():
            parts = [buf[f"grad_{k}"][...].reshape(width, ROUNDS[k][1]) for k in range(n_rounds)]
            return parts[0] if len(parts) == 1 else jnp.concatenate(parts, axis=1)

        owned = jnp.int32(0)
        for j in range(nb_all):
            owned = owned + jnp.where(owners_ref[0, j] == me, 1, 0)
        mine = owned > 0
        tall = 128
        per = tall // strip
        pre, arrived = buf["pre"], buf["arrived"]

        def give(to):
            pltpu.make_async_remote_copy(
                src_ref=pre.at[to], dst_ref=arrived.at[me], send_sem=a2a_send.at[n_rounds],
                recv_sem=a2a_recv.at[n_rounds], device_id=(to, ten), device_id_type=MESH,
            ).start()

        squares = jnp.zeros((8, width), F32)
        for i in range(width // tall):
            rows = pl.ds(i * tall, tall)
            p = jnp.dot(buf["half"][rows, :], buf["rroot"][...], preferred_element_type=F32)
            pre[pl.ds(i * per, per)] = p.astype(BF16).reshape(per, strip, width)
            squares = squares + jnp.sum((p * p).reshape(tall // 8, 8, width), axis=0)
            if GIVE == "early":
                def some(o, _, i=i):
                    to = i * per + lax.rem(me + o, per)

                    @pl.when(to != me)
                    def _():
                        give(to)

                    return 0

                lax.fori_loop(0, per, some, 0)
        def give_to(spans):
            for first, last in spans:
                lax.fori_loop(first, last, lambda o, _: (give(peer(o)), 0)[1], 0)

        if GIVE == "split":
            give_to(FIRST)
        arrived[me] = pre[me]

        grad_squares = jnp.sum(buf["gsq"][...], axis=0)
        count = width * width
        grad_mean = jnp.sum(grad_squares, axis=(0, 1), keepdims=True) / count
        pre_mean = jnp.sum(squares, axis=(0, 1), keepdims=True) / count
        factor = jnp.sqrt(grad_mean + epsilon) / jnp.sqrt(pre_mean + epsilon)
        share = (pre_mean / (pre_mean + epsilon)) * (grad_mean + epsilon) * count
        owned, block = jnp.int32(0), jnp.int32(0)
        for j in range(nb_all):
            here = owners_ref[0, j] == me
            owned = owned + jnp.where(here, 1, 0)
            block = jnp.where(here, j, block)
        mine = owned > 0
        share = lax.select(mine, share, jnp.zeros_like(share))
        factor = lax.select(mine, factor, jnp.zeros_like(factor))

        def exchange(ref, n, dev, at, value):
            ref[0] = value
            for o in range(1, n):
                pltpu.make_async_remote_copy(
                    src_ref=ref.at[0], dst_ref=ref.at[o], send_sem=sum_send.at[at], recv_sem=sum_recv.at[at],
                    device_id=dev(o), device_id_type=MESH,
                ).start()

            def finish():
                if n > 1:
                    part = ref.at[pl.ds(1, n - 1)]
                    pltpu.make_async_copy(part, part, sum_recv.at[at]).wait()
                return jnp.sum(ref[...], axis=0)

            return finish

        finish = exchange(buf["sum_t"], n_tensor, lambda o: (me, lax.rem(ten + o, n_tensor)), 0,
                          jnp.broadcast_to(share, (8, 128)))
        if GIVE == "near":
            lax.fori_loop(1, n_dp, lambda o, _: (give(peer(o)), 0)[1], 0)
        if GIVE == "far":
            lax.fori_loop(1, n_dp, lambda o, _: (give(peer(n_dp - o)), 0)[1], 0)

        lanes = lax.broadcasted_iota(jnp.int32, (8, 128), 1)
        in_row = lax.broadcasted_iota(jnp.int32, (8, 128), 0) == block
        local = jnp.where(lanes < 64, jnp.where(in_row, jnp.broadcast_to(factor, (8, 128)), 0.0), finish())
        finish = exchange(buf["sum_y"], NY, lambda o: (z * NY + lax.rem(y + o, NY), ten), 1, local)
        finish = exchange(buf["sum_z"], nz, lambda o: (lax.rem(z + o, nz) * NY + y, ten), 2, finish())
        if GIVE == "split":
            give_to(LAST)

        gram_weight = (1.0 - decay_rate) / width

        def statistic(factor_ref, gram):
            add = gram_weight * gram
            add = lax.select(mine, add, jnp.zeros_like(add))
            return decay_rate * factor_ref + add

        for i in range(width // tall):
            rows = pl.ds(i * tall, tall)
            gram = jnp.zeros((tall, width), F32)
            for k in range(n_rounds):
                gk = buf[f"grad_{k}"]
                per = tall // strip
                top = gk[pl.ds(i * per, per)].reshape(tall, ROUNDS[k][1])
                gram = gram + lax.dot_general(top, gk[...].reshape(width, ROUNDS[k][1]), (((1,), (1,)), ((), ())),
                                              preferred_element_type=F32)
            nl_ref[rows, :] = statistic(buf["lfac"][rows, :], gram)
        grad = whole()
        flipped = grad.T
        for i in range(width // tall):
            rows = pl.ds(i * tall, tall)
            gram = jnp.dot(flipped[i * tall:(i + 1) * tall], grad, preferred_element_type=F32)
            nr_ref[rows, :] = statistic(buf["rfac"][rows, :], gram)
        for c in copies.values():
            c.wait_send()
        for k in range(n_rounds):
            a2a_all(a2a_send.at[k], buf[f"stage_{k}"]).wait()

        entries = nb_all * n_tensor * width * width
        norms = finish()
        scale = 1.0 / jnp.sqrt(norms[0:1, 64:65] / entries + epsilon)
        for at, (n, ref) in enumerate(((n_tensor, buf["sum_t"]), (NY, buf["sum_y"]), (nz, buf["sum_z"]))):
            if n > 1:
                part = ref.at[pl.ds(1, n - 1)]
                pltpu.make_async_copy(part, part, sum_send.at[at]).wait()
        scale = jnp.broadcast_to(scale, (strip, width))
        a2a_all(a2a_recv.at[n_rounds], arrived).wait()
        for j in range(nb_all):
            shaped = arrived[owners_ref[0, j]].astype(F32) * jnp.broadcast_to(norms[j:j + 1, 0:1], (strip, width))
            dir_ref[j] = (shaped * scale).astype(BF16)
        a2a_all(a2a_send.at[n_rounds], pre).wait()

    hbm = pl.BlockSpec(memory_space=pl.ANY)
    vmem = pl.BlockSpec(memory_space=pltpu.VMEM)
    new_left, new_right, directions = pl.pallas_call(
        kernel,
        out_shape=(
            pltpu.VMEM((width, width), F32),
            pltpu.VMEM((width, width), F32),
            pltpu.VMEM((nb_all, strip, width), BF16),
        ),
        in_specs=[pl.BlockSpec(memory_space=pltpu.SMEM)] + [hbm] * 5,
        out_specs=(vmem, vmem, vmem),
        scratch_shapes=shapes
        + [
            pltpu.SemaphoreType.DMA((n_msg,)),
            pltpu.SemaphoreType.DMA((n_msg,)),
            pltpu.SemaphoreType.DMA((n_rounds,)),
            pltpu.SemaphoreType.DMA((4,)),
            pltpu.SemaphoreType.DMA((n_rounds + 1,)),
            pltpu.SemaphoreType.DMA((n_rounds + 1,)),
            pltpu.SemaphoreType.DMA((3,)),
            pltpu.SemaphoreType.DMA((3,)),
        ],
        compiler_params=pltpu.CompilerParams(
            collective_id=0, has_side_effects=True, vmem_limit_bytes=58 * 1024 * 1024
        ),
        name="shampoo",
    )(owners, g, left_factor[0, 0], right_factor[0, 0], left_root[0, 0], right_root[0, 0])
    return new_left[None, None], new_right[None, None], directions


def solution(mesh):
    nz = mesh.shape["dp"] // NY
    return jax.shard_map(
        functools.partial(per_device, nz, mesh.shape["tensor"]),
        mesh=mesh,
        in_specs=(
            P("dp", "tensor", None, None),
            P("tensor", None),
            P("tensor", "dp", None, None),
            P("tensor", "dp", None, None),
            P("tensor", "dp", None, None),
            P("tensor", "dp", None, None),
        ),
        out_specs=(
            P("tensor", "dp", None, None),
            P("tensor", "dp", None, None),
            P("tensor", "dp", None),
        ),
        check_vma=False,
    )
```

```python
import functools

import jax
import jax.numpy as jnp
from jax import lax
from jax.experimental import pallas as pl
from jax.experimental.pallas import tpu as pltpu
from jax.sharding import PartitionSpec as P

MESH = pl.DeviceIdType.MESH
F32 = jnp.float32
BF16 = jnp.bfloat16
decay_rate = 0.95
epsilon = 1e-06
NY = 4

ROUNDS = (
    (0, 128, (
        (4, "y", 1, "ct", 13.1),
        (3, "y", -1, "cc", 6.5),
        (1, "z", 1, "cd", 7.2),
    )),
    (128, 256, (
        (2, "y", -1, "ct", 15.8),
        (3, "z", 1, "cd", 12.0),
        (2, "z", -1, "cd", 21.6),
        (1, "y", 1, "cd", 16.8),
    )),
    (384, 128, (
        (4, "y", -1, "cd", 29.3),
        (3, "z", 1, "cd", 19.8),
        (1, "y", 1, "cd", 21.2),
    )),
)
FULL = False
FOLD = 0.002
YFAR = (1, -1, 2)
ZFAR = (1, -1, 2, -2, 3, -3, 4)
MODEL = (46.5, 2.2, 3.0)


class Whole:
    def __init__(self, ref, send, recv):
        self.ref, self.send, self.recv = ref, send, recv

    def wait_recv(self):
        pltpu.make_async_copy(self.ref, self.ref, self.recv).wait()

    def wait_send(self):
        pltpu.make_async_copy(self.ref, self.ref, self.send).wait()


def plan(events, rate, latency, lead):
    free = dict.fromkeys([(a, q) for a in "yz" for q in (1, -1)], 0.0)
    arrive, done, order, now = {}, {}, [], 0.0
    left = list(events)
    while left:
        best = None
        for e in left:
            if any(m not in arrive for m in e["needs"]) or any(d not in done for d in e["after"]):
                continue
            ready = max([arrive[m] for m in e["needs"]] + [now])
            if not e["needs"] and not e["after"]:
                ready = max([now] + [free[link] - lead for _, link, _ in e["sends"]])
            key = (ready, e["rank"])
            if best is None or key < best[0]:
                best = (key, e)
        (ready, _), e = best
        now = ready + e["cost"]
        for name, link, kib in e["sends"]:
            free[link] = max(free[link], now) + kib * 1.024 / rate
            arrive[name] = free[link] + latency
        done[e["name"]] = now
        order.append(e)
        left.remove(e)
    return order, now


def per_device(nz, n_tensor, gradients, owners, left_factor, right_factor, left_root, right_root):
    nb_all, width = gradients.shape[1], gradients.shape[2]
    n_dp = nz * NY
    strip = width // n_dp
    g = gradients.reshape(nb_all, nz, NY, strip, width)
    sets = []
    for k, (c0, w, found) in enumerate(ROUNDS):
        b0 = 0
        for nb, axis, s, forms, rank in found:
            sets.append((k, c0, w, b0, nb, axis == "y", s, (forms, rank)))
            b0 += nb
    names, shapes = [], []

    def buffer(name, shape, dtype=BF16):
        names.append(name)
        shapes.append(pltpu.VMEM(shape, dtype))

    messages = {}
    half = nz // 2
    for i, (k, c0, w, b0, nb, yfirst, s, forms) in enumerate(sets):
        ychunk = (nb, nz, strip, w) if yfirst else (nb, strip, w)
        zchunk = (nb, strip, w) if yfirst else (nb, NY, strip, w)
        forms = forms[0]
        yform, zform = forms if yfirst else forms[::-1]
        buffer(("mid", i), ychunk if yfirst else zchunk)
        if yform == "c":
            for n in ("ry1", "ry2", "ry3", "sy"):
                buffer((n, i), ychunk)
            found = [("y1",), ("y2",), ("y3",)]
        else:
            buffer(("ry", i), (NY - 1,) + ychunk)
            found = [("y",)]
        if zform == "c":
            buffer(("rza", i), (half,) + zchunk)
            buffer(("rzb", i), (half - 1,) + zchunk)
            buffer(("sza", i), (half - 1,) + zchunk)
            buffer(("szb", i), (half - 2,) + zchunk)
            found += [("a", h) for h in range(half)] + [("b", h) for h in range(half - 1)]
        elif zform == "t":
            buffer(("rt", i), (7,) + zchunk)
            buffer(("st", i), (2,) + zchunk)
            found += [("t", h) for h in range(7)]
        else:
            buffer(("rz", i), (nz - 1,) + zchunk)
            found += [("z",)]
        for n in found:
            messages[n + (i,)] = len(messages)
    for k, (c0, w, _) in enumerate(ROUNDS):
        buffer(("agg", k), (nb_all, strip, w))
        buffer(("stage", k), (n_dp, strip, w))
        buffer(("grad", k), (n_dp, strip, w))
    buffer("own", (nb_all, nz, NY, strip, width))
    buffer("lroot", (width, width))
    buffer("rroot", (width, width))
    buffer("lfac", (width, width), F32)
    buffer("rfac", (width, width), F32)
    buffer("pre", (n_dp, strip, width))
    buffer("half", (width, width))
    buffer("gsq", (len(ROUNDS), 8, 128), F32)
    buffer("arrived", (n_dp, strip, width))
    buffer("sum_t", (n_tensor, 8, 128), F32)
    buffer("sum_y", (NY, 8, 128), F32)
    buffer("sum_z", (nz, 8, 128), F32)

    n_msg = len(messages)
    n_rounds = len(ROUNDS)

    def kernel(owners_ref, g_ref, lf_ref, rf_ref, lr_ref, rr_ref, nl_ref, nr_ref, dir_ref, *scratch):
        buf = dict(zip(names, scratch))
        send, recv, own_sem, load_sem, a2a_send, a2a_recv, sum_send, sum_recv = scratch[len(names):]
        me, ten = lax.axis_index("dp"), lax.axis_index("tensor")
        z, y = me // NY, me % NY

        def zat(d):
            return lax.rem(z + d + 2 * nz, nz)

        def yat(d):
            return lax.rem(y + d + 2 * NY, NY)

        def zdev(d):
            return (zat(d) * NY + y, ten)

        def ydev(d):
            return (z * NY + yat(d), ten)

        barrier = pltpu.get_barrier_semaphore()

        met = [ydev(d) for d in (1, -1, 2)] + [zdev(d) for d in (1, -1, 2, -2, 3, -3, 4)]
        met += [(me, lax.rem(ten + o, n_tensor)) for o in range(1, n_tensor)]
        if FULL:
            met += [(zat(dz) * NY + yat(dy), ten) for dz in range(1, nz) for dy in range(1, NY)]

        def greet():
            for dev in met:
                pl.semaphore_signal(barrier, inc=1, device_id=dev, device_id_type=MESH)
            pl.semaphore_wait(barrier, len(met))

        own_copies = []
        for k, (c0, w, _) in enumerate(ROUNDS):
            cols = pl.ds(c0, w)
            own_copies.append(
                pltpu.make_async_copy(
                    g_ref.at[:, :, :, :, cols], buf["own"].at[:, :, :, :, cols], own_sem.at[k]
                )
            )
        loads = [
            pltpu.make_async_copy(lr_ref, buf["lroot"], load_sem.at[0]),
            pltpu.make_async_copy(rr_ref, buf["rroot"], load_sem.at[1]),
            pltpu.make_async_copy(lf_ref, buf["lfac"], load_sem.at[2]),
            pltpu.make_async_copy(rf_ref, buf["rfac"], load_sem.at[3]),
        ]
        copies = {}

        def put(name, src, dst, dev):
            i = messages[name]
            copies[name] = pltpu.make_async_remote_copy(
                src_ref=src, dst_ref=dst, send_sem=send.at[i], recv_sem=recv.at[i],
                device_id=dev, device_id_type=MESH,
            )
            copies[name].start()

        def total(parts):
            if len(parts) == 2:
                return parts[0] + parts[1]
            acc = parts[0].astype(F32)
            for p in parts[1:]:
                acc = acc + p.astype(F32)
            return acc.astype(BF16)

        events = []

        def event(name, emit, rank, needs=(), after=(), sends=(), cost=0.2):
            events.append(dict(name=name, emit=emit, rank=rank, needs=needs, after=after, sends=sends, cost=cost))

        loaded = set()

        def need_own(k):
            if k not in loaded:
                loaded.add(k)
                own_copies[k].wait()

        finals = {k: [] for k in range(n_rounds)}
        for i, (k, c0, w, b0, nb, yfirst, s, forms) in enumerate(sets):
            forms, rank = forms
            yform, zform = forms if yfirst else forms[::-1]
            cols = pl.ds(c0, w)
            blocks = pl.ds(b0, nb)
            kib = nb * strip * w * 2 / 1024

            def own_y(src, i=i, blocks=blocks, cols=cols, yfirst=yfirst):
                return (lambda d: src.at[blocks, :, yat(d), :, cols]) if yfirst else (lambda d: src.at[:, yat(d)])

            def own_z(src, i=i, blocks=blocks, cols=cols, yfirst=yfirst):
                return (lambda d: src.at[:, zat(d)]) if yfirst else (lambda d: src.at[blocks, zat(d), :, :, cols])

            def fold(dst, parts, lead, n_lead, nb=nb):
                if not lead:
                    for b in range(nb):
                        dst[b] = total([p[b] for p in parts])
                    return

                def one(v, _):
                    for b in range(nb):
                        dst[b, v] = total([p[b, v] for p in parts])
                    return 0

                lax.fori_loop(0, n_lead, one, 0)

            first_y, first_z = yfirst, not yfirst
            ysize = kib * nz if yfirst else kib
            zsize = kib if yfirst else kib * NY
            mid = buf[("mid", i)]
            y_raw = own_y(g_ref if yfirst else mid)
            y_own = own_y(buf["own"] if yfirst else mid)
            z_raw = own_z(mid if yfirst else g_ref)
            z_own = own_z(mid if yfirst else buf["own"])
            agg = buf[("agg", k)].at[blocks]
            ry1, ry2, ry3, sy = (buf.get((n, i)) for n in ("ry1", "ry2", "ry3", "sy"))
            rza, rzb, sza, szb = (buf.get((n, i)) for n in ("rza", "rzb", "sza", "szb"))
            ry, rz = buf.get(("ry", i)), buf.get(("rz", i))
            rt, st = buf.get(("rt", i)), buf.get(("st", i))
            ylead = (yfirst, nz)
            zlead = (not yfirst, NY)
            up, down = s, -s
            yl, zl = {1: ("y", s), -1: ("y", -s)}, {1: ("z", s), -1: ("z", -s)}
            yk, zk = (rank, k * 10 + 5) if yfirst else (k * 10 + 5, rank)
            yr, zr = (k * 10, zk) if yfirst else (yk, k * 10)
            ybase = () if yfirst else (("zd", i),)
            zbase = (("yd", i),) if yfirst else ()

            def y0(i=i, y_raw=y_raw, ry1=ry1, ry3=ry3, s=s):
                put(("y1", i), y_raw(2 * s), ry1, ydev(s))
                put(("y3", i), y_raw(-s), ry3, ydev(-s))

            def y1(i=i, k=k, y_own=y_own, ry1=ry1, ry2=ry2, sy=sy, s=s, fold=fold, ylead=ylead):
                need_own(k)
                copies[("y1", i)].wait_recv()
                fold(sy, [ry1, y_own(s)], *ylead)
                put(("y2", i), sy, ry2, ydev(s))

            def y2(i=i, k=k, y_own=y_own, ry2=ry2, ry3=ry3, fold=fold, ylead=ylead,
                   dst=mid if yfirst else agg):
                need_own(k)
                copies[("y2", i)].wait_recv()
                copies[("y3", i)].wait_recv()
                fold(dst, [ry2, ry3, y_own(0)], *ylead)

            def straight(name, raw, into, far, dev):
                i = messages[name]
                for at, d in enumerate(far):
                    pltpu.make_async_remote_copy(
                        src_ref=raw(d), dst_ref=into.at[at], send_sem=send.at[i], recv_sem=recv.at[i],
                        device_id=dev(d), device_id_type=MESH,
                    ).start()
                copies[name] = Whole(into, send.at[i], recv.at[i])

            def ystart(i=i, y_raw=y_raw, ry=ry, straight=straight):
                straight(("y", i), y_raw, ry, YFAR, ydev)

            def yend(i=i, k=k, y_own=y_own, ry=ry, fold=fold, ylead=ylead, dst=mid if yfirst else agg):
                need_own(k)
                copies[("y", i)].wait_recv()
                fold(dst, [y_own(0)] + [ry.at[at] for at in range(NY - 1)], *ylead)

            def zflood(i=i, z_raw=z_raw, rz=rz, straight=straight):
                straight(("z", i), z_raw, rz, ZFAR, zdev)

            def zsink(i=i, k=k, z_own=z_own, rz=rz, fold=fold, zlead=zlead, dst=agg if yfirst else mid):
                need_own(k)
                copies[("z", i)].wait_recv()
                fold(dst, [z_own(0)] + [rz.at[at] for at in range(nz - 1)], *zlead)

            def zpairs(i=i, z_raw=z_raw, rt=rt, s=s):
                for at, (chunk, to) in enumerate(((4, 2), (3, 1), (-3, -1), (1, 1), (-1, -1))):
                    put(("t", at, i), z_raw(chunk * s), rt.at[at], zdev(to * s))

            def zjoin(i=i, k=k, z_own=z_own, rt=rt, st=st, s=s, fold=fold, zlead=zlead):
                need_own(k)
                for at in range(3):
                    copies[("t", at, i)].wait_recv()
                fold(st.at[0], [rt.at[0], rt.at[1], z_own(2 * s)], *zlead)
                put(("t", 5, i), st.at[0], rt.at[5], zdev(2 * s))
                fold(st.at[1], [rt.at[2], z_own(-2 * s)], *zlead)
                put(("t", 6, i), st.at[1], rt.at[6], zdev(-2 * s))

            def zmeet(i=i, k=k, z_own=z_own, rt=rt, fold=fold, zlead=zlead, dst=agg if yfirst else mid):
                need_own(k)
                for at in range(3, 7):
                    copies[("t", at, i)].wait_recv()
                fold(dst, [z_own(0)] + [rt.at[at] for at in range(3, 7)], *zlead)

            if yform == "c":
                event(("y0", i), y0, yk, after=ybase,
                      sends=[(("y1", i), yl[1], ysize), (("y3", i), yl[-1], ysize)])
                event(("y1", i), y1, yr - 1, needs=[("y1", i)], sends=[(("y2", i), yl[1], ysize)], cost=0.1 + FOLD * ysize * 2)
                event(("yd", i), y2, yr - 2, needs=[("y2", i), ("y3", i)], cost=0.1 + FOLD * ysize * 3)
            else:
                event(("y0", i), ystart, yk, after=ybase,
                      sends=[(("y+", i), yl[1], 2 * ysize), (("y-", i), yl[-1], 2 * ysize)])
                event(("yd", i), yend, yr - 2, needs=[("y+", i), ("y-", i)], cost=0.1 + FOLD * ysize * 4)
            if zform == "t":
                event(("z0", i), zpairs, zk, after=zbase,
                      sends=[(("t+", i), zl[1], 3 * zsize), (("t-", i), zl[-1], zsize),
                             (("T+", i), zl[1], zsize), (("T-", i), zl[-1], zsize)])
                event(("z1", i), zjoin, zr - 1, needs=[("t+", i), ("t-", i)],
                      sends=[(("u+", i), zl[1], 2 * zsize), (("u-", i), zl[-1], 2 * zsize)], cost=0.2 + FOLD * zsize * 5)
                event(("zd", i), zmeet, zr - 2, needs=[("u+", i), ("u-", i), ("T+", i), ("T-", i)],
                      cost=0.1 + FOLD * zsize * 5)
            if zform == "d":
                event(("z0", i), zflood, zk, after=zbase,
                      sends=[(("z+", i), zl[1], 8 * zsize), (("z-", i), zl[-1], 8 * zsize)])
                event(("zd", i), zsink, zr - 2, needs=[("z+", i), ("z-", i)], cost=0.1 + FOLD * zsize * 8)

            def zstart(i=i, z_raw=z_raw, rza=rza, rzb=rzb, s=s):
                put(("a", 0, i), z_raw(half * s), rza.at[0], zdev(s))
                put(("b", 0, i), z_raw(-(half - 1) * s), rzb.at[0], zdev(-s))

            if zform == "c":
                event(("z0", i), zstart, zk, after=zbase,
                      sends=[(("a", 0, i), zl[1], zsize), (("b", 0, i), zl[-1], zsize)])
                for h in range(1, half):
                    def za(i=i, k=k, h=h, z_own=z_own, rza=rza, sza=sza, s=s, fold=fold, zlead=zlead):
                        need_own(k)
                        copies[("a", h - 1, i)].wait_recv()
                        fold(sza.at[h - 1], [rza.at[h - 1], z_own((half - h) * s)], *zlead)
                        put(("a", h, i), sza.at[h - 1], rza.at[h], zdev(s))

                    event(("za", h, i), za, zr - 1, needs=[("a", h - 1, i)], sends=[(("a", h, i), zl[1], zsize)],
                          cost=0.1 + FOLD * zsize * 2)
                for h in range(1, half - 1):
                    def zb(i=i, k=k, h=h, z_own=z_own, rzb=rzb, szb=szb, s=s, fold=fold, zlead=zlead):
                        need_own(k)
                        copies[("b", h - 1, i)].wait_recv()
                        fold(szb.at[h - 1], [rzb.at[h - 1], z_own(-(half - 1 - h) * s)], *zlead)
                        put(("b", h, i), szb.at[h - 1], rzb.at[h], zdev(-s))

                    event(("zb", h, i), zb, zr - 1, needs=[("b", h - 1, i)], sends=[(("b", h, i), zl[-1], zsize)],
                          cost=0.1 + FOLD * zsize * 2)

                def zend(i=i, k=k, z_own=z_own, rza=rza, rzb=rzb, fold=fold, zlead=zlead,
                         dst=agg if yfirst else mid):
                    need_own(k)
                    copies[("a", half - 1, i)].wait_recv()
                    copies[("b", half - 2, i)].wait_recv()
                    fold(dst, [rza.at[half - 1], rzb.at[half - 2], z_own(0)], *zlead)

                event(("zd", i), zend, zr - 2, needs=[("a", half - 1, i), ("b", half - 2, i)],
                      cost=0.1 + FOLD * zsize * 3)
            finals[k].append(("zd", i) if yfirst else ("yd", i))

        def block_of(device):
            found = jnp.int32(0)
            for j in range(nb_all):
                found = jnp.where(owners_ref[0, j] == device, j, found)
            return found

        def peer(o):
            dz, dy = o // NY, o % NY
            step = jnp.where(dz % 2 == 1, (dz + 1) // 2, nz - dz // 2)
            return lax.rem(z + step, nz) * NY + lax.rem(y + dy, NY)

        for k, (c0, w, _) in enumerate(ROUNDS):
            kib = strip * w * 2 / 1024

            def route(k=k):
                agg, stage, grad = (buf[(n, k)] for n in ("agg", "stage", "grad"))

                def one(o, _):
                    to = peer(o)
                    stage[o] = agg[block_of(to)]
                    pltpu.make_async_remote_copy(
                        src_ref=stage.at[o], dst_ref=grad.at[me], send_sem=a2a_send.at[k], recv_sem=a2a_recv.at[k],
                        device_id=(to, ten), device_id_type=MESH,
                    ).start()
                    return 0

                lax.fori_loop(1, n_dp, one, 0)
                grad[me] = agg[block_of(me)]

            event(("route", k), route, k * 10 - 3, after=finals[k],
                  sends=[(("rz", q, k), ("z", q), kib * 8 * NY) for q in (1, -1)]
                  + [(("ry", q, k), ("y", q), kib * 2 * nz) for q in (1, -1)], cost=1.7)

        def a2a_all(sem, ref):
            part = ref.at[pl.ds(0, n_dp - 1)]
            return pltpu.make_async_copy(part, part, sem)

        waited = []

        def land(k):
            a2a_all(a2a_recv.at[k], buf[("grad", k)]).wait()
            if not waited:
                waited.append(k)
                for c in loads:
                    c.wait()
            w = ROUNDS[k][1]
            gk = buf[("grad", k)][...].reshape(width, w)
            buf["half"][:, ROUNDS[k][0]:ROUNDS[k][0] + w] = jnp.dot(
                buf["lroot"][...], gk, preferred_element_type=F32).astype(BF16)
            gf = gk.astype(F32)
            folded = jnp.sum((gf * gf).reshape(width // 8, 8, w), axis=0)
            buf["gsq"][k] = sum(folded[:, c:c + 128] for c in range(0, w, 128))

        for k in range(n_rounds):
            event(("land", k), functools.partial(land, k), k * 10 - 4,
                  needs=[("rz", q, k) for q in (1, -1)] + [("ry", q, k) for q in (1, -1)], cost=0.7)

        for c in own_copies:
            c.start()
        greet()
        order, _ = plan(events, *MODEL)
        started = False
        for e in order:
            if not started and (e["needs"] or e is order[-1]):
                started = True
                for c in loads:
                    c.start()
            e["emit"]()


        def whole():
            parts = [buf[("grad", k)][...].reshape(width, ROUNDS[k][1]) for k in range(n_rounds)]
            return parts[0] if len(parts) == 1 else jnp.concatenate(parts, axis=1)

        owned = jnp.int32(0)
        for j in range(nb_all):
            owned = owned + jnp.where(owners_ref[0, j] == me, 1, 0)
        mine = owned > 0
        tall = 128
        per = tall // strip
        pre, arrived = buf["pre"], buf["arrived"]

        def give(to):
            pltpu.make_async_remote_copy(
                src_ref=pre.at[to], dst_ref=arrived.at[me], send_sem=a2a_send.at[n_rounds],
                recv_sem=a2a_recv.at[n_rounds], device_id=(to, ten), device_id_type=MESH,
            ).start()

        squares = jnp.zeros((8, width), F32)
        for i in range(width // tall):
            rows = pl.ds(i * tall, tall)
            p = jnp.dot(buf["half"][rows, :], buf["rroot"][...], preferred_element_type=F32)
            pre[pl.ds(i * per, per)] = p.astype(BF16).reshape(per, strip, width)
            squares = squares + jnp.sum((p * p).reshape(tall // 8, 8, width), axis=0)
        arrived[me] = pre[me]

        grad_squares = jnp.sum(buf["gsq"][...], axis=0)
        count = width * width
        grad_mean = jnp.sum(grad_squares, axis=(0, 1), keepdims=True) / count
        pre_mean = jnp.sum(squares, axis=(0, 1), keepdims=True) / count
        factor = jnp.sqrt(grad_mean + epsilon) / jnp.sqrt(pre_mean + epsilon)
        share = (pre_mean / (pre_mean + epsilon)) * (grad_mean + epsilon) * count
        owned, block = jnp.int32(0), jnp.int32(0)
        for j in range(nb_all):
            here = owners_ref[0, j] == me
            owned = owned + jnp.where(here, 1, 0)
            block = jnp.where(here, j, block)
        mine = owned > 0
        share = lax.select(mine, share, jnp.zeros_like(share))
        factor = lax.select(mine, factor, jnp.zeros_like(factor))

        def exchange(ref, n, dev, at, value):
            ref[0] = value
            for o in range(1, n):
                pltpu.make_async_remote_copy(
                    src_ref=ref.at[0], dst_ref=ref.at[o], send_sem=sum_send.at[at], recv_sem=sum_recv.at[at],
                    device_id=dev(o), device_id_type=MESH,
                ).start()

            def finish():
                if n > 1:
                    part = ref.at[pl.ds(1, n - 1)]
                    pltpu.make_async_copy(part, part, sum_recv.at[at]).wait()
                return jnp.sum(ref[...], axis=0)

            return finish

        finish = exchange(buf["sum_t"], n_tensor, lambda o: (me, lax.rem(ten + o, n_tensor)), 0,
                          jnp.broadcast_to(share, (8, 128)))
        lax.fori_loop(1, n_dp, lambda o, _: (give(peer(o)), 0)[1], 0)

        lanes = lax.broadcasted_iota(jnp.int32, (8, 128), 1)
        in_row = lax.broadcasted_iota(jnp.int32, (8, 128), 0) == block
        local = jnp.where(lanes < 64, jnp.where(in_row, jnp.broadcast_to(factor, (8, 128)), 0.0), finish())
        finish = exchange(buf["sum_y"], NY, lambda o: (z * NY + lax.rem(y + o, NY), ten), 1, local)
        finish = exchange(buf["sum_z"], nz, lambda o: (lax.rem(z + o, nz) * NY + y, ten), 2, finish())

        gram_weight = (1.0 - decay_rate) / width

        def statistic(factor_ref, gram):
            add = gram_weight * gram
            add = lax.select(mine, add, jnp.zeros_like(add))
            return decay_rate * factor_ref + add

        for i in range(width // tall):
            rows = pl.ds(i * tall, tall)
            gram = jnp.zeros((tall, width), F32)
            for k in range(n_rounds):
                gk = buf[("grad", k)]
                per = tall // strip
                top = gk[pl.ds(i * per, per)].reshape(tall, ROUNDS[k][1])
                gram = gram + lax.dot_general(top, gk[...].reshape(width, ROUNDS[k][1]), (((1,), (1,)), ((), ())),
                                              preferred_element_type=F32)
            nl_ref[rows, :] = statistic(buf["lfac"][rows, :], gram)
        grad = whole()
        flipped = grad.T
        for i in range(width // tall):
            rows = pl.ds(i * tall, tall)
            gram = jnp.dot(flipped[i * tall:(i + 1) * tall], grad, preferred_element_type=F32)
            nr_ref[rows, :] = statistic(buf["rfac"][rows, :], gram)
        for c in copies.values():
            c.wait_send()
        for k in range(n_rounds):
            a2a_all(a2a_send.at[k], buf[("stage", k)]).wait()

        entries = nb_all * n_tensor * width * width
        norms = finish()
        scale = 1.0 / jnp.sqrt(norms[0:1, 64:65] / entries + epsilon)
        for at, (n, ref) in enumerate(((n_tensor, buf["sum_t"]), (NY, buf["sum_y"]), (nz, buf["sum_z"]))):
            if n > 1:
                part = ref.at[pl.ds(1, n - 1)]
                pltpu.make_async_copy(part, part, sum_send.at[at]).wait()
        scale = jnp.broadcast_to(scale, (strip, width))
        a2a_all(a2a_recv.at[n_rounds], arrived).wait()
        for j in range(nb_all):
            shaped = arrived[owners_ref[0, j]].astype(F32) * jnp.broadcast_to(norms[j:j + 1, 0:1], (strip, width))
            dir_ref[j] = (shaped * scale).astype(BF16)
        a2a_all(a2a_send.at[n_rounds], pre).wait()

    hbm = pl.BlockSpec(memory_space=pl.ANY)
    vmem = pl.BlockSpec(memory_space=pltpu.VMEM)
    new_left, new_right, directions = pl.pallas_call(
        kernel,
        out_shape=(
            pltpu.VMEM((width, width), F32),
            pltpu.VMEM((width, width), F32),
            pltpu.VMEM((nb_all, strip, width), BF16),
        ),
        in_specs=[pl.BlockSpec(memory_space=pltpu.SMEM)] + [hbm] * 5,
        out_specs=(vmem, vmem, vmem),
        scratch_shapes=shapes
        + [
            pltpu.SemaphoreType.DMA((n_msg,)),
            pltpu.SemaphoreType.DMA((n_msg,)),
            pltpu.SemaphoreType.DMA((n_rounds,)),
            pltpu.SemaphoreType.DMA((4,)),
            pltpu.SemaphoreType.DMA((n_rounds + 1,)),
            pltpu.SemaphoreType.DMA((n_rounds + 1,)),
            pltpu.SemaphoreType.DMA((3,)),
            pltpu.SemaphoreType.DMA((3,)),
        ],
        compiler_params=pltpu.CompilerParams(
            collective_id=0, has_side_effects=True, vmem_limit_bytes=58 * 1024 * 1024
        ),
        name="shampoo",
    )(owners, g, left_factor[0, 0], right_factor[0, 0], left_root[0, 0], right_root[0, 0])
    return new_left[None, None], new_right[None, None], directions


def solution(mesh):
    nz = mesh.shape["dp"] // NY
    return jax.shard_map(
        functools.partial(per_device, nz, mesh.shape["tensor"]),
        mesh=mesh,
        in_specs=(
            P("dp", "tensor", None, None),
            P("tensor", None),
            P("tensor", "dp", None, None),
            P("tensor", "dp", None, None),
            P("tensor", "dp", None, None),
            P("tensor", "dp", None, None),
        ),
        out_specs=(
            P("tensor", "dp", None, None),
            P("tensor", "dp", None, None),
            P("tensor", "dp", None),
        ),
        check_vma=False,
    )
```

```python
import functools

import jax
import jax.numpy as jnp
from jax import lax
from jax.experimental import pallas as pl
from jax.experimental.pallas import tpu as pltpu
from jax.sharding import PartitionSpec as P

MESH = pl.DeviceIdType.MESH
F32 = jnp.float32
BF16 = jnp.bfloat16
decay_rate = 0.95
epsilon = 1e-06
NY = 4

ROUNDS = (
    (0, 256, (
        (1, "y", 1, "cd", -6.07),
        (3, "y", -1, "ct", 8.4),
        (3, "y", 1, "ct", 11.2),
        (1, "z", 1, "cd", -1.16),
    )),
    (256, 128, (
        (3, "z", -1, "cd", 14.79),
        (5, "z", 1, "cd", 12.9),
    )),
    (384, 128, (
        (5, "z", -1, "cd", 25.3),
        (2, "y", -1, "cd", 11.75),
        (1, "y", -1, "cd", 27.9),
    )),
)
FULL = False
FOLD = 0.002
YFAR = (1, -1, 2)
ZFAR = (1, -1, 2, -2, 3, -3, 4)
MODEL = (47.5, 2.0, 3.0)


class Whole:
    def __init__(self, ref, send, recv):
        self.ref, self.send, self.recv = ref, send, recv

    def wait_recv(self):
        pltpu.make_async_copy(self.ref, self.ref, self.recv).wait()

    def wait_send(self):
        pltpu.make_async_copy(self.ref, self.ref, self.send).wait()


def plan(events, rate, latency, lead):
    free = dict.fromkeys([(a, q) for a in "yz" for q in (1, -1)], 0.0)
    arrive, done, order, now = {}, {}, [], 0.0
    left = list(events)
    while left:
        best = None
        for e in left:
            if any(m not in arrive for m in e["needs"]) or any(d not in done for d in e["after"]):
                continue
            ready = max([arrive[m] for m in e["needs"]] + [now])
            if not e["needs"] and not e["after"]:
                ready = max([now] + [free[link] - lead for _, link, _ in e["sends"]])
            key = (ready, e["rank"])
            if best is None or key < best[0]:
                best = (key, e)
        (ready, _), e = best
        now = ready + e["cost"]
        for name, link, kib in e["sends"]:
            free[link] = max(free[link], now) + kib * 1.024 / rate
            arrive[name] = free[link] + latency
        done[e["name"]] = now
        order.append(e)
        left.remove(e)
    return order, now


def per_device(nz, n_tensor, gradients, owners, left_factor, right_factor, left_root, right_root):
    nb_all, width = gradients.shape[1], gradients.shape[2]
    n_dp = nz * NY
    strip = width // n_dp
    g = gradients.reshape(nb_all, nz, NY, strip, width)
    sets = []
    for k, (c0, w, found) in enumerate(ROUNDS):
        b0 = 0
        for nb, axis, s, forms, rank in found:
            sets.append((k, c0, w, b0, nb, axis == "y", s, (forms, rank)))
            b0 += nb
    names, shapes = [], []

    def buffer(name, shape, dtype=BF16):
        names.append(name)
        shapes.append(pltpu.VMEM(shape, dtype))

    messages = {}
    half = nz // 2
    for i, (k, c0, w, b0, nb, yfirst, s, forms) in enumerate(sets):
        ychunk = (nb, nz, strip, w) if yfirst else (nb, strip, w)
        zchunk = (nb, strip, w) if yfirst else (nb, NY, strip, w)
        forms = forms[0]
        yform, zform = forms if yfirst else forms[::-1]
        buffer(("mid", i), ychunk if yfirst else zchunk)
        if yform == "c":
            for n in ("ry1", "ry2", "ry3", "sy"):
                buffer((n, i), ychunk)
            found = [("y1",), ("y2",), ("y3",)]
        else:
            buffer(("ry", i), (NY - 1,) + ychunk)
            found = [("y",)]
        if zform == "c":
            buffer(("rza", i), (half,) + zchunk)
            buffer(("rzb", i), (half - 1,) + zchunk)
            buffer(("sza", i), (half - 1,) + zchunk)
            buffer(("szb", i), (half - 2,) + zchunk)
            found += [("a", h) for h in range(half)] + [("b", h) for h in range(half - 1)]
        elif zform == "t":
            buffer(("rt", i), (7,) + zchunk)
            buffer(("st", i), (2,) + zchunk)
            found += [("t", h) for h in range(7)]
        else:
            buffer(("rz", i), (nz - 1,) + zchunk)
            found += [("z",)]
        for n in found:
            messages[n + (i,)] = len(messages)
    for k, (c0, w, _) in enumerate(ROUNDS):
        buffer(("agg", k), (nb_all, strip, w))
        buffer(("stage", k), (n_dp, strip, w))
        buffer(("grad", k), (n_dp, strip, w))
    buffer("own", (nb_all, nz, NY, strip, width))
    buffer("lroot", (width, width))
    buffer("rroot", (width, width))
    buffer("lfac", (width, width), F32)
    buffer("rfac", (width, width), F32)
    buffer("pre", (n_dp, strip, width))
    buffer("half", (width, width))
    buffer("turned", (width, width))
    buffer("gsq", (len(ROUNDS), 8, 128), F32)
    buffer("arrived", (n_dp, strip, width))
    buffer("sum_t", (n_tensor, 8, 128), F32)
    buffer("sum_y", (NY, 8, 128), F32)
    buffer("sum_z", (nz, 8, 128), F32)

    n_msg = len(messages)
    n_rounds = len(ROUNDS)

    def kernel(owners_ref, g_ref, lf_ref, rf_ref, lr_ref, rr_ref, nl_ref, nr_ref, dir_ref, *scratch):
        buf = dict(zip(names, scratch))
        send, recv, own_sem, load_sem, a2a_send, a2a_recv, sum_send, sum_recv = scratch[len(names):]
        me, ten = lax.axis_index("dp"), lax.axis_index("tensor")
        z, y = me // NY, me % NY

        def zat(d):
            return lax.rem(z + d + 2 * nz, nz)

        def yat(d):
            return lax.rem(y + d + 2 * NY, NY)

        def zdev(d):
            return (zat(d) * NY + y, ten)

        def ydev(d):
            return (z * NY + yat(d), ten)

        barrier = pltpu.get_barrier_semaphore()

        met = [ydev(d) for d in (1, -1, 2)] + [zdev(d) for d in (1, -1, 2, -2, 3, -3, 4)]
        met += [(me, lax.rem(ten + o, n_tensor)) for o in range(1, n_tensor)]
        if FULL:
            met += [(zat(dz) * NY + yat(dy), ten) for dz in range(1, nz) for dy in range(1, NY)]

        def greet():
            for dev in met:
                pl.semaphore_signal(barrier, inc=1, device_id=dev, device_id_type=MESH)
            pl.semaphore_wait(barrier, len(met))

        own_copies = []
        for k, (c0, w, _) in enumerate(ROUNDS):
            cols = pl.ds(c0, w)
            own_copies.append(
                pltpu.make_async_copy(
                    g_ref.at[:, :, :, :, cols], buf["own"].at[:, :, :, :, cols], own_sem.at[k]
                )
            )
        loads = [
            pltpu.make_async_copy(lr_ref, buf["lroot"], load_sem.at[0]),
            pltpu.make_async_copy(rr_ref, buf["rroot"], load_sem.at[1]),
            pltpu.make_async_copy(lf_ref, buf["lfac"], load_sem.at[2]),
            pltpu.make_async_copy(rf_ref, buf["rfac"], load_sem.at[3]),
        ]
        copies = {}

        def put(name, src, dst, dev):
            i = messages[name]
            copies[name] = pltpu.make_async_remote_copy(
                src_ref=src, dst_ref=dst, send_sem=send.at[i], recv_sem=recv.at[i],
                device_id=dev, device_id_type=MESH,
            )
            copies[name].start()

        def total(parts):
            if len(parts) == 2:
                return parts[0] + parts[1]
            acc = parts[0].astype(F32)
            for p in parts[1:]:
                acc = acc + p.astype(F32)
            return acc.astype(BF16)

        events = []

        def event(name, emit, rank, needs=(), after=(), sends=(), cost=0.2):
            events.append(dict(name=name, emit=emit, rank=rank, needs=needs, after=after, sends=sends, cost=cost))

        loaded = set()

        def need_own(k):
            if k not in loaded:
                loaded.add(k)
                own_copies[k].wait()

        finals = {k: [] for k in range(n_rounds)}
        for i, (k, c0, w, b0, nb, yfirst, s, forms) in enumerate(sets):
            forms, rank = forms
            yform, zform = forms if yfirst else forms[::-1]
            cols = pl.ds(c0, w)
            blocks = pl.ds(b0, nb)
            kib = nb * strip * w * 2 / 1024

            def own_y(src, i=i, blocks=blocks, cols=cols, yfirst=yfirst):
                return (lambda d: src.at[blocks, :, yat(d), :, cols]) if yfirst else (lambda d: src.at[:, yat(d)])

            def own_z(src, i=i, blocks=blocks, cols=cols, yfirst=yfirst):
                return (lambda d: src.at[:, zat(d)]) if yfirst else (lambda d: src.at[blocks, zat(d), :, :, cols])

            def fold(dst, parts, lead, n_lead, nb=nb):
                if not lead:
                    for b in range(nb):
                        dst[b] = total([p[b] for p in parts])
                    return

                def one(v, _):
                    for b in range(nb):
                        dst[b, v] = total([p[b, v] for p in parts])
                    return 0

                lax.fori_loop(0, n_lead, one, 0)

            first_y, first_z = yfirst, not yfirst
            ysize = kib * nz if yfirst else kib
            zsize = kib if yfirst else kib * NY
            mid = buf[("mid", i)]
            y_raw = own_y(g_ref if yfirst else mid)
            y_own = own_y(buf["own"] if yfirst else mid)
            z_raw = own_z(mid if yfirst else g_ref)
            z_own = own_z(mid if yfirst else buf["own"])
            agg = buf[("agg", k)].at[blocks]
            ry1, ry2, ry3, sy = (buf.get((n, i)) for n in ("ry1", "ry2", "ry3", "sy"))
            rza, rzb, sza, szb = (buf.get((n, i)) for n in ("rza", "rzb", "sza", "szb"))
            ry, rz = buf.get(("ry", i)), buf.get(("rz", i))
            rt, st = buf.get(("rt", i)), buf.get(("st", i))
            ylead = (yfirst, nz)
            zlead = (not yfirst, NY)
            up, down = s, -s
            yl, zl = {1: ("y", s), -1: ("y", -s)}, {1: ("z", s), -1: ("z", -s)}
            yk, zk = (rank, k * 10 + 5) if yfirst else (k * 10 + 5, rank)
            yr, zr = (k * 10, zk) if yfirst else (yk, k * 10)
            ybase = () if yfirst else (("zd", i),)
            zbase = (("yd", i),) if yfirst else ()

            def y0(i=i, y_raw=y_raw, ry1=ry1, ry3=ry3, s=s):
                put(("y1", i), y_raw(2 * s), ry1, ydev(s))
                put(("y3", i), y_raw(-s), ry3, ydev(-s))

            def y1(i=i, k=k, y_own=y_own, ry1=ry1, ry2=ry2, sy=sy, s=s, fold=fold, ylead=ylead):
                need_own(k)
                copies[("y1", i)].wait_recv()
                fold(sy, [ry1, y_own(s)], *ylead)
                put(("y2", i), sy, ry2, ydev(s))

            def y2(i=i, k=k, y_own=y_own, ry2=ry2, ry3=ry3, fold=fold, ylead=ylead,
                   dst=mid if yfirst else agg):
                need_own(k)
                copies[("y2", i)].wait_recv()
                copies[("y3", i)].wait_recv()
                fold(dst, [ry2, ry3, y_own(0)], *ylead)

            def straight(name, raw, into, far, dev):
                i = messages[name]
                for at, d in enumerate(far):
                    pltpu.make_async_remote_copy(
                        src_ref=raw(d), dst_ref=into.at[at], send_sem=send.at[i], recv_sem=recv.at[i],
                        device_id=dev(d), device_id_type=MESH,
                    ).start()
                copies[name] = Whole(into, send.at[i], recv.at[i])

            def ystart(i=i, y_raw=y_raw, ry=ry, straight=straight):
                straight(("y", i), y_raw, ry, YFAR, ydev)

            def yend(i=i, k=k, y_own=y_own, ry=ry, fold=fold, ylead=ylead, dst=mid if yfirst else agg):
                need_own(k)
                copies[("y", i)].wait_recv()
                fold(dst, [y_own(0)] + [ry.at[at] for at in range(NY - 1)], *ylead)

            def zflood(i=i, z_raw=z_raw, rz=rz, straight=straight):
                straight(("z", i), z_raw, rz, ZFAR, zdev)

            def zsink(i=i, k=k, z_own=z_own, rz=rz, fold=fold, zlead=zlead, dst=agg if yfirst else mid):
                need_own(k)
                copies[("z", i)].wait_recv()
                fold(dst, [z_own(0)] + [rz.at[at] for at in range(nz - 1)], *zlead)

            def zpairs(i=i, z_raw=z_raw, rt=rt, s=s):
                for at, (chunk, to) in enumerate(((4, 2), (3, 1), (-3, -1), (1, 1), (-1, -1))):
                    put(("t", at, i), z_raw(chunk * s), rt.at[at], zdev(to * s))

            def zjoin(i=i, k=k, z_own=z_own, rt=rt, st=st, s=s, fold=fold, zlead=zlead):
                need_own(k)
                for at in range(3):
                    copies[("t", at, i)].wait_recv()
                fold(st.at[0], [rt.at[0], rt.at[1], z_own(2 * s)], *zlead)
                put(("t", 5, i), st.at[0], rt.at[5], zdev(2 * s))
                fold(st.at[1], [rt.at[2], z_own(-2 * s)], *zlead)
                put(("t", 6, i), st.at[1], rt.at[6], zdev(-2 * s))

            def zmeet(i=i, k=k, z_own=z_own, rt=rt, fold=fold, zlead=zlead, dst=agg if yfirst else mid):
                need_own(k)
                for at in range(3, 7):
                    copies[("t", at, i)].wait_recv()
                fold(dst, [z_own(0)] + [rt.at[at] for at in range(3, 7)], *zlead)

            if yform == "c":
                event(("y0", i), y0, yk, after=ybase,
                      sends=[(("y1", i), yl[1], ysize), (("y3", i), yl[-1], ysize)])
                event(("y1", i), y1, yr - 1, needs=[("y1", i)], sends=[(("y2", i), yl[1], ysize)], cost=0.1 + FOLD * ysize * 2)
                event(("yd", i), y2, yr - 2, needs=[("y2", i), ("y3", i)], cost=0.1 + FOLD * ysize * 3)
            else:
                event(("y0", i), ystart, yk, after=ybase,
                      sends=[(("y+", i), yl[1], 2 * ysize), (("y-", i), yl[-1], 2 * ysize)])
                event(("yd", i), yend, yr - 2, needs=[("y+", i), ("y-", i)], cost=0.1 + FOLD * ysize * 4)
            if zform == "t":
                event(("z0", i), zpairs, zk, after=zbase,
                      sends=[(("t+", i), zl[1], 3 * zsize), (("t-", i), zl[-1], zsize),
                             (("T+", i), zl[1], zsize), (("T-", i), zl[-1], zsize)])
                event(("z1", i), zjoin, zr - 1, needs=[("t+", i), ("t-", i)],
                      sends=[(("u+", i), zl[1], 2 * zsize), (("u-", i), zl[-1], 2 * zsize)], cost=0.2 + FOLD * zsize * 5)
                event(("zd", i), zmeet, zr - 2, needs=[("u+", i), ("u-", i), ("T+", i), ("T-", i)],
                      cost=0.1 + FOLD * zsize * 5)
            if zform == "d":
                event(("z0", i), zflood, zk, after=zbase,
                      sends=[(("z+", i), zl[1], 8 * zsize), (("z-", i), zl[-1], 8 * zsize)])
                event(("zd", i), zsink, zr - 2, needs=[("z+", i), ("z-", i)], cost=0.1 + FOLD * zsize * 8)

            def zstart(i=i, z_raw=z_raw, rza=rza, rzb=rzb, s=s):
                put(("a", 0, i), z_raw(half * s), rza.at[0], zdev(s))
                put(("b", 0, i), z_raw(-(half - 1) * s), rzb.at[0], zdev(-s))

            if zform == "c":
                event(("z0", i), zstart, zk, after=zbase,
                      sends=[(("a", 0, i), zl[1], zsize), (("b", 0, i), zl[-1], zsize)])
                for h in range(1, half):
                    def za(i=i, k=k, h=h, z_own=z_own, rza=rza, sza=sza, s=s, fold=fold, zlead=zlead):
                        need_own(k)
                        copies[("a", h - 1, i)].wait_recv()
                        fold(sza.at[h - 1], [rza.at[h - 1], z_own((half - h) * s)], *zlead)
                        put(("a", h, i), sza.at[h - 1], rza.at[h], zdev(s))

                    event(("za", h, i), za, zr - 1, needs=[("a", h - 1, i)], sends=[(("a", h, i), zl[1], zsize)],
                          cost=0.1 + FOLD * zsize * 2)
                for h in range(1, half - 1):
                    def zb(i=i, k=k, h=h, z_own=z_own, rzb=rzb, szb=szb, s=s, fold=fold, zlead=zlead):
                        need_own(k)
                        copies[("b", h - 1, i)].wait_recv()
                        fold(szb.at[h - 1], [rzb.at[h - 1], z_own(-(half - 1 - h) * s)], *zlead)
                        put(("b", h, i), szb.at[h - 1], rzb.at[h], zdev(-s))

                    event(("zb", h, i), zb, zr - 1, needs=[("b", h - 1, i)], sends=[(("b", h, i), zl[-1], zsize)],
                          cost=0.1 + FOLD * zsize * 2)

                def zend(i=i, k=k, z_own=z_own, rza=rza, rzb=rzb, fold=fold, zlead=zlead,
                         dst=agg if yfirst else mid):
                    need_own(k)
                    copies[("a", half - 1, i)].wait_recv()
                    copies[("b", half - 2, i)].wait_recv()
                    fold(dst, [rza.at[half - 1], rzb.at[half - 2], z_own(0)], *zlead)

                event(("zd", i), zend, zr - 2, needs=[("a", half - 1, i), ("b", half - 2, i)],
                      cost=0.1 + FOLD * zsize * 3)
            finals[k].append(("zd", i) if yfirst else ("yd", i))

        def block_of(device):
            found = jnp.int32(0)
            for j in range(nb_all):
                found = jnp.where(owners_ref[0, j] == device, j, found)
            return found

        def peer(o):
            dz, dy = o // NY, o % NY
            step = jnp.where(dz % 2 == 1, (dz + 1) // 2, nz - dz // 2)
            return lax.rem(z + step, nz) * NY + lax.rem(y + dy, NY)

        for k, (c0, w, _) in enumerate(ROUNDS):
            kib = strip * w * 2 / 1024

            def route(k=k):
                agg, stage, grad = (buf[(n, k)] for n in ("agg", "stage", "grad"))

                def one(o, _):
                    to = peer(o)
                    stage[o] = agg[block_of(to)]
                    pltpu.make_async_remote_copy(
                        src_ref=stage.at[o], dst_ref=grad.at[me], send_sem=a2a_send.at[k], recv_sem=a2a_recv.at[k],
                        device_id=(to, ten), device_id_type=MESH,
                    ).start()
                    return 0

                lax.fori_loop(1, n_dp, one, 0)
                grad[me] = agg[block_of(me)]

            event(("route", k), route, k * 10 - 3, after=finals[k],
                  sends=[(("rz", q, k), ("z", q), kib * 8 * NY) for q in (1, -1)]
                  + [(("ry", q, k), ("y", q), kib * 2 * nz) for q in (1, -1)], cost=1.7)

        def a2a_all(sem, ref):
            part = ref.at[pl.ds(0, n_dp - 1)]
            return pltpu.make_async_copy(part, part, sem)

        waited = []

        def land(k):
            a2a_all(a2a_recv.at[k], buf[("grad", k)]).wait()
            if not waited:
                waited.append(k)
                for c in loads:
                    c.wait()
            w = ROUNDS[k][1]
            gk = buf[("grad", k)][...].reshape(width, w)
            buf["half"][:, ROUNDS[k][0]:ROUNDS[k][0] + w] = jnp.dot(
                buf["lroot"][...], gk, preferred_element_type=F32).astype(BF16)
            gf = gk.astype(F32)
            folded = jnp.sum((gf * gf).reshape(width // 8, 8, w), axis=0)
            buf["gsq"][k] = sum(folded[:, c:c + 128] for c in range(0, w, 128))

        for k in range(n_rounds):
            event(("land", k), functools.partial(land, k), k * 10 - 4,
                  needs=[("rz", q, k) for q in (1, -1)] + [("ry", q, k) for q in (1, -1)], cost=0.7)

        for c in own_copies:
            c.start()
        greet()
        order, _ = plan(events, *MODEL)
        started = False
        for e in order:
            if not started and (e["needs"] or e is order[-1]):
                started = True
                for c in loads:
                    c.start()
            e["emit"]()


        def whole():
            parts = [buf[("grad", k)][...].reshape(width, ROUNDS[k][1]) for k in range(n_rounds)]
            return parts[0] if len(parts) == 1 else jnp.concatenate(parts, axis=1)

        owned = jnp.int32(0)
        for j in range(nb_all):
            owned = owned + jnp.where(owners_ref[0, j] == me, 1, 0)
        mine = owned > 0
        tall = 128
        per = tall // strip
        pre, arrived = buf["pre"], buf["arrived"]

        def give(to):
            pltpu.make_async_remote_copy(
                src_ref=pre.at[to], dst_ref=arrived.at[me], send_sem=a2a_send.at[n_rounds],
                recv_sem=a2a_recv.at[n_rounds], device_id=(to, ten), device_id_type=MESH,
            ).start()

        squares = jnp.zeros((8, width), F32)
        for i in range(width // tall):
            rows = pl.ds(i * tall, tall)
            p = jnp.dot(buf["half"][rows, :], buf["rroot"][...], preferred_element_type=F32)
            pre[pl.ds(i * per, per)] = p.astype(BF16).reshape(per, strip, width)
            squares = squares + jnp.sum((p * p).reshape(tall // 8, 8, width), axis=0)
        arrived[me] = pre[me]

        grad_squares = jnp.sum(buf["gsq"][...], axis=0)
        count = width * width
        grad_mean = jnp.sum(grad_squares, axis=(0, 1), keepdims=True) / count
        pre_mean = jnp.sum(squares, axis=(0, 1), keepdims=True) / count
        factor = jnp.sqrt(grad_mean + epsilon) / jnp.sqrt(pre_mean + epsilon)
        share = (pre_mean / (pre_mean + epsilon)) * (grad_mean + epsilon) * count
        owned, block = jnp.int32(0), jnp.int32(0)
        for j in range(nb_all):
            here = owners_ref[0, j] == me
            owned = owned + jnp.where(here, 1, 0)
            block = jnp.where(here, j, block)
        mine = owned > 0
        share = lax.select(mine, share, jnp.zeros_like(share))
        factor = lax.select(mine, factor, jnp.zeros_like(factor))

        def exchange(ref, n, dev, at, value):
            ref[0] = value
            for o in range(1, n):
                pltpu.make_async_remote_copy(
                    src_ref=ref.at[0], dst_ref=ref.at[o], send_sem=sum_send.at[at], recv_sem=sum_recv.at[at],
                    device_id=dev(o), device_id_type=MESH,
                ).start()

            def finish():
                if n > 1:
                    part = ref.at[pl.ds(1, n - 1)]
                    pltpu.make_async_copy(part, part, sum_recv.at[at]).wait()
                return jnp.sum(ref[...], axis=0)

            return finish

        finish = exchange(buf["sum_t"], n_tensor, lambda o: (me, lax.rem(ten + o, n_tensor)), 0,
                          jnp.broadcast_to(share, (8, 128)))
        lax.fori_loop(1, n_dp, lambda o, _: (give(peer(o)), 0)[1], 0)

        lanes = lax.broadcasted_iota(jnp.int32, (8, 128), 1)
        in_row = lax.broadcasted_iota(jnp.int32, (8, 128), 0) == block
        local = jnp.where(lanes < 64, jnp.where(in_row, jnp.broadcast_to(factor, (8, 128)), 0.0), finish())
        finish = exchange(buf["sum_y"], NY, lambda o: (z * NY + lax.rem(y + o, NY), ten), 1, local)
        finish = exchange(buf["sum_z"], nz, lambda o: (lax.rem(z + o, nz) * NY + y, ten), 2, finish())

        gram_weight = (1.0 - decay_rate) / width

        def statistic(factor_ref, gram):
            add = gram_weight * gram
            add = lax.select(mine, add, jnp.zeros_like(add))
            return decay_rate * factor_ref + add

        grad = whole()
        flipped = grad.T
        buf["turned"][...] = flipped

        def left_rows(i, _):
            rows = pl.ds(i * tall, tall)
            gram = jnp.zeros((tall, width), F32)
            for k, (c0, w, _) in enumerate(ROUNDS):
                top = buf[("grad", k)][pl.ds(i * per, per)].reshape(tall, w)
                gram = gram + jnp.dot(top, buf["turned"][c0:c0 + w, :], preferred_element_type=F32)
            nl_ref[rows, :] = statistic(buf["lfac"][rows, :], gram)
            return 0

        lax.fori_loop(0, width // tall, left_rows, 0)
        def right_rows(i, _):
            rows = pl.ds(i * tall, tall)
            for k, (c0, w, _) in enumerate(ROUNDS):
                gram = jnp.dot(buf["turned"][rows, :], buf[("grad", k)][...].reshape(width, w), preferred_element_type=F32)
                nr_ref[rows, c0:c0 + w] = statistic(buf["rfac"][rows, c0:c0 + w], gram)
            return 0

        lax.fori_loop(0, width // tall, right_rows, 0)
        for c in copies.values():
            c.wait_send()
        for k in range(n_rounds):
            a2a_all(a2a_send.at[k], buf[("stage", k)]).wait()

        entries = nb_all * n_tensor * width * width
        norms = finish()
        scale = 1.0 / jnp.sqrt(norms[0:1, 64:65] / entries + epsilon)
        for at, (n, ref) in enumerate(((n_tensor, buf["sum_t"]), (NY, buf["sum_y"]), (nz, buf["sum_z"]))):
            if n > 1:
                part = ref.at[pl.ds(1, n - 1)]
                pltpu.make_async_copy(part, part, sum_send.at[at]).wait()
        scale = jnp.broadcast_to(scale, (strip, width))
        a2a_all(a2a_recv.at[n_rounds], arrived).wait()
        for j in range(nb_all):
            shaped = arrived[owners_ref[0, j]].astype(F32) * jnp.broadcast_to(norms[j:j + 1, 0:1], (strip, width))
            dir_ref[j] = (shaped * scale).astype(BF16)
        a2a_all(a2a_send.at[n_rounds], pre).wait()

    hbm = pl.BlockSpec(memory_space=pl.ANY)
    vmem = pl.BlockSpec(memory_space=pltpu.VMEM)
    new_left, new_right, directions = pl.pallas_call(
        kernel,
        out_shape=(
            pltpu.VMEM((width, width), F32),
            pltpu.VMEM((width, width), F32),
            pltpu.VMEM((nb_all, strip, width), BF16),
        ),
        in_specs=[pl.BlockSpec(memory_space=pltpu.SMEM)] + [hbm] * 5,
        out_specs=(vmem, vmem, vmem),
        scratch_shapes=shapes
        + [
            pltpu.SemaphoreType.DMA((n_msg,)),
            pltpu.SemaphoreType.DMA((n_msg,)),
            pltpu.SemaphoreType.DMA((n_rounds,)),
            pltpu.SemaphoreType.DMA((4,)),
            pltpu.SemaphoreType.DMA((n_rounds + 1,)),
            pltpu.SemaphoreType.DMA((n_rounds + 1,)),
            pltpu.SemaphoreType.DMA((3,)),
            pltpu.SemaphoreType.DMA((3,)),
        ],
        compiler_params=pltpu.CompilerParams(
            collective_id=0, has_side_effects=True, vmem_limit_bytes=58 * 1024 * 1024
        ),
        name="shampoo",
    )(owners, g, left_factor[0, 0], right_factor[0, 0], left_root[0, 0], right_root[0, 0])
    return new_left[None, None], new_right[None, None], directions


def solution(mesh):
    nz = mesh.shape["dp"] // NY
    return jax.shard_map(
        functools.partial(per_device, nz, mesh.shape["tensor"]),
        mesh=mesh,
        in_specs=(
            P("dp", "tensor", None, None),
            P("tensor", None),
            P("tensor", "dp", None, None),
            P("tensor", "dp", None, None),
            P("tensor", "dp", None, None),
            P("tensor", "dp", None, None),
        ),
        out_specs=(
            P("tensor", "dp", None, None),
            P("tensor", "dp", None, None),
            P("tensor", "dp", None),
        ),
        check_vma=False,
    )
```

```python
import functools

import jax
import jax.numpy as jnp
from jax import lax
from jax.experimental import pallas as pl
from jax.experimental.pallas import tpu as pltpu
from jax.sharding import PartitionSpec as P

MESH = pl.DeviceIdType.MESH
F32 = jnp.float32
BF16 = jnp.bfloat16
decay_rate = 0.95
epsilon = 1e-06
NY = 4

ROUNDS = (
    (0, 256, (
        (1, "y", 1, "cd", -6.07),
        (3, "y", -1, "ct", 8.4),
        (3, "y", 1, "ct", 11.2),
        (1, "z", 1, "cd", -6.03),
    )),
    (256, 128, (
        (3, "z", -1, "cd", 19.4),
        (5, "z", 1, "cd", 12.9),
    )),
    (384, 128, (
        (5, "z", -1, "cd", 25.3),
        (1, "y", -1, "cd", 13.09),
        (2, "y", -1, "cd", 19.2),
    )),
)
FIRST = ((4, 32),)
LAST = ((1, 4),)
FULL = False
FOLD = 0.002
YFAR = (1, -1, 2)
ZFAR = (1, -1, 2, -2, 3, -3, 4)
MODEL = (47.5, 2.0, 3.0)


class Whole:
    def __init__(self, ref, send, recv):
        self.ref, self.send, self.recv = ref, send, recv

    def wait_recv(self):
        pltpu.make_async_copy(self.ref, self.ref, self.recv).wait()

    def wait_send(self):
        pltpu.make_async_copy(self.ref, self.ref, self.send).wait()


def plan(events, rate, latency, lead):
    free = dict.fromkeys([(a, q) for a in "yz" for q in (1, -1)], 0.0)
    arrive, done, order, now = {}, {}, [], 0.0
    left = list(events)
    while left:
        best = None
        for e in left:
            if any(m not in arrive for m in e["needs"]) or any(d not in done for d in e["after"]):
                continue
            ready = max([arrive[m] for m in e["needs"]] + [now])
            if not e["needs"] and not e["after"]:
                ready = max([now] + [free[link] - lead for _, link, _ in e["sends"]])
            key = (ready, e["rank"])
            if best is None or key < best[0]:
                best = (key, e)
        (ready, _), e = best
        now = ready + e["cost"]
        for name, link, kib in e["sends"]:
            free[link] = max(free[link], now) + kib * 1.024 / rate
            arrive[name] = free[link] + latency
        done[e["name"]] = now
        order.append(e)
        left.remove(e)
    return order, now


def per_device(nz, n_tensor, gradients, owners, left_factor, right_factor, left_root, right_root):
    nb_all, width = gradients.shape[1], gradients.shape[2]
    n_dp = nz * NY
    strip = width // n_dp
    g = gradients.reshape(nb_all, nz, NY, strip, width)
    sets = []
    for k, (c0, w, found) in enumerate(ROUNDS):
        b0 = 0
        for nb, axis, s, forms, rank in found:
            sets.append((k, c0, w, b0, nb, axis == "y", s, (forms, rank)))
            b0 += nb
    names, shapes = [], []

    def buffer(name, shape, dtype=BF16):
        names.append(name)
        shapes.append(pltpu.VMEM(shape, dtype))

    messages = {}
    half = nz // 2
    for i, (k, c0, w, b0, nb, yfirst, s, forms) in enumerate(sets):
        ychunk = (nb, nz, strip, w) if yfirst else (nb, strip, w)
        zchunk = (nb, strip, w) if yfirst else (nb, NY, strip, w)
        forms = forms[0]
        yform, zform = forms if yfirst else forms[::-1]
        buffer(("mid", i), ychunk if yfirst else zchunk)
        if yform == "c":
            for n in ("ry1", "ry2", "ry3", "sy"):
                buffer((n, i), ychunk)
            found = [("y1",), ("y2",), ("y3",)]
        else:
            buffer(("ry", i), (NY - 1,) + ychunk)
            found = [("y",)]
        if zform == "c":
            buffer(("rza", i), (half,) + zchunk)
            buffer(("rzb", i), (half - 1,) + zchunk)
            buffer(("sza", i), (half - 1,) + zchunk)
            buffer(("szb", i), (half - 2,) + zchunk)
            found += [("a", h) for h in range(half)] + [("b", h) for h in range(half - 1)]
        elif zform == "t":
            buffer(("rt", i), (7,) + zchunk)
            buffer(("st", i), (2,) + zchunk)
            found += [("t", h) for h in range(7)]
        else:
            buffer(("rz", i), (nz - 1,) + zchunk)
            found += [("z",)]
        for n in found:
            messages[n + (i,)] = len(messages)
    for k, (c0, w, _) in enumerate(ROUNDS):
        buffer(("agg", k), (nb_all, strip, w))
        buffer(("stage", k), (n_dp, strip, w))
        buffer(("grad", k), (n_dp, strip, w))
    buffer("own", (nb_all, nz, NY, strip, width))
    buffer("lroot", (width, width))
    buffer("rroot", (width, width))
    buffer("lfac", (width, width), F32)
    buffer("rfac", (width, width), F32)
    buffer("pre", (n_dp, strip, width))
    buffer("half", (width, width))
    buffer("turned", (width, width))
    buffer("gsq", (len(ROUNDS), 8, 128), F32)
    buffer("arrived", (n_dp, strip, width))
    buffer("sum_t", (n_tensor, 8, 128), F32)
    buffer("sum_y", (NY, 8, 128), F32)
    buffer("sum_z", (nz, 8, 128), F32)

    n_msg = len(messages)
    n_rounds = len(ROUNDS)

    def kernel(owners_ref, g_ref, lf_ref, rf_ref, lr_ref, rr_ref, nl_ref, nr_ref, dir_ref, *scratch):
        buf = dict(zip(names, scratch))
        send, recv, own_sem, load_sem, a2a_send, a2a_recv, sum_send, sum_recv = scratch[len(names):]
        me, ten = lax.axis_index("dp"), lax.axis_index("tensor")
        z, y = me // NY, me % NY

        def zat(d):
            return lax.rem(z + d + 2 * nz, nz)

        def yat(d):
            return lax.rem(y + d + 2 * NY, NY)

        def zdev(d):
            return (zat(d) * NY + y, ten)

        def ydev(d):
            return (z * NY + yat(d), ten)

        barrier = pltpu.get_barrier_semaphore()

        met = [ydev(d) for d in (1, -1, 2)] + [zdev(d) for d in (1, -1, 2, -2, 3, -3, 4)]
        met += [(me, lax.rem(ten + o, n_tensor)) for o in range(1, n_tensor)]
        if FULL:
            met += [(zat(dz) * NY + yat(dy), ten) for dz in range(1, nz) for dy in range(1, NY)]

        def greet():
            for dev in met:
                pl.semaphore_signal(barrier, inc=1, device_id=dev, device_id_type=MESH)
            pl.semaphore_wait(barrier, len(met))

        own_copies = []
        for k, (c0, w, _) in enumerate(ROUNDS):
            cols = pl.ds(c0, w)
            own_copies.append(
                pltpu.make_async_copy(
                    g_ref.at[:, :, :, :, cols], buf["own"].at[:, :, :, :, cols], own_sem.at[k]
                )
            )
        loads = [
            pltpu.make_async_copy(lr_ref, buf["lroot"], load_sem.at[0]),
            pltpu.make_async_copy(rr_ref, buf["rroot"], load_sem.at[1]),
            pltpu.make_async_copy(lf_ref, buf["lfac"], load_sem.at[2]),
            pltpu.make_async_copy(rf_ref, buf["rfac"], load_sem.at[3]),
        ]
        copies = {}

        def put(name, src, dst, dev):
            i = messages[name]
            copies[name] = pltpu.make_async_remote_copy(
                src_ref=src, dst_ref=dst, send_sem=send.at[i], recv_sem=recv.at[i],
                device_id=dev, device_id_type=MESH,
            )
            copies[name].start()

        def total(parts):
            if len(parts) == 2:
                return parts[0] + parts[1]
            acc = parts[0].astype(F32)
            for p in parts[1:]:
                acc = acc + p.astype(F32)
            return acc.astype(BF16)

        events = []

        def event(name, emit, rank, needs=(), after=(), sends=(), cost=0.2):
            events.append(dict(name=name, emit=emit, rank=rank, needs=needs, after=after, sends=sends, cost=cost))

        loaded = set()

        def need_own(k):
            if k not in loaded:
                loaded.add(k)
                own_copies[k].wait()

        finals = {k: [] for k in range(n_rounds)}
        for i, (k, c0, w, b0, nb, yfirst, s, forms) in enumerate(sets):
            forms, rank = forms
            yform, zform = forms if yfirst else forms[::-1]
            cols = pl.ds(c0, w)
            blocks = pl.ds(b0, nb)
            kib = nb * strip * w * 2 / 1024

            def own_y(src, i=i, blocks=blocks, cols=cols, yfirst=yfirst):
                return (lambda d: src.at[blocks, :, yat(d), :, cols]) if yfirst else (lambda d: src.at[:, yat(d)])

            def own_z(src, i=i, blocks=blocks, cols=cols, yfirst=yfirst):
                return (lambda d: src.at[:, zat(d)]) if yfirst else (lambda d: src.at[blocks, zat(d), :, :, cols])

            def fold(dst, parts, lead, n_lead, nb=nb):
                if not lead:
                    for b in range(nb):
                        dst[b] = total([p[b] for p in parts])
                    return

                def one(v, _):
                    for b in range(nb):
                        dst[b, v] = total([p[b, v] for p in parts])
                    return 0

                lax.fori_loop(0, n_lead, one, 0)

            first_y, first_z = yfirst, not yfirst
            ysize = kib * nz if yfirst else kib
            zsize = kib if yfirst else kib * NY
            mid = buf[("mid", i)]
            y_raw = own_y(g_ref if yfirst else mid)
            y_own = own_y(buf["own"] if yfirst else mid)
            z_raw = own_z(mid if yfirst else g_ref)
            z_own = own_z(mid if yfirst else buf["own"])
            agg = buf[("agg", k)].at[blocks]
            ry1, ry2, ry3, sy = (buf.get((n, i)) for n in ("ry1", "ry2", "ry3", "sy"))
            rza, rzb, sza, szb = (buf.get((n, i)) for n in ("rza", "rzb", "sza", "szb"))
            ry, rz = buf.get(("ry", i)), buf.get(("rz", i))
            rt, st = buf.get(("rt", i)), buf.get(("st", i))
            ylead = (yfirst, nz)
            zlead = (not yfirst, NY)
            up, down = s, -s
            yl, zl = {1: ("y", s), -1: ("y", -s)}, {1: ("z", s), -1: ("z", -s)}
            yk, zk = (rank, k * 10 + 5) if yfirst else (k * 10 + 5, rank)
            yr, zr = (k * 10, zk) if yfirst else (yk, k * 10)
            ybase = () if yfirst else (("zd", i),)
            zbase = (("yd", i),) if yfirst else ()

            def y0(i=i, y_raw=y_raw, ry1=ry1, ry3=ry3, s=s):
                put(("y1", i), y_raw(2 * s), ry1, ydev(s))
                put(("y3", i), y_raw(-s), ry3, ydev(-s))

            def y1(i=i, k=k, y_own=y_own, ry1=ry1, ry2=ry2, sy=sy, s=s, fold=fold, ylead=ylead):
                need_own(k)
                copies[("y1", i)].wait_recv()
                fold(sy, [ry1, y_own(s)], *ylead)
                put(("y2", i), sy, ry2, ydev(s))

            def y2(i=i, k=k, y_own=y_own, ry2=ry2, ry3=ry3, fold=fold, ylead=ylead,
                   dst=mid if yfirst else agg):
                need_own(k)
                copies[("y2", i)].wait_recv()
                copies[("y3", i)].wait_recv()
                fold(dst, [ry2, ry3, y_own(0)], *ylead)

            def straight(name, raw, into, far, dev):
                i = messages[name]
                for at, d in enumerate(far):
                    pltpu.make_async_remote_copy(
                        src_ref=raw(d), dst_ref=into.at[at], send_sem=send.at[i], recv_sem=recv.at[i],
                        device_id=dev(d), device_id_type=MESH,
                    ).start()
                copies[name] = Whole(into, send.at[i], recv.at[i])

            def ystart(i=i, y_raw=y_raw, ry=ry, straight=straight):
                straight(("y", i), y_raw, ry, YFAR, ydev)

            def yend(i=i, k=k, y_own=y_own, ry=ry, fold=fold, ylead=ylead, dst=mid if yfirst else agg):
                need_own(k)
                copies[("y", i)].wait_recv()
                fold(dst, [y_own(0)] + [ry.at[at] for at in range(NY - 1)], *ylead)

            def zflood(i=i, z_raw=z_raw, rz=rz, straight=straight):
                straight(("z", i), z_raw, rz, ZFAR, zdev)

            def zsink(i=i, k=k, z_own=z_own, rz=rz, fold=fold, zlead=zlead, dst=agg if yfirst else mid):
                need_own(k)
                copies[("z", i)].wait_recv()
                fold(dst, [z_own(0)] + [rz.at[at] for at in range(nz - 1)], *zlead)

            def zpairs(i=i, z_raw=z_raw, rt=rt, s=s):
                for at, (chunk, to) in enumerate(((4, 2), (3, 1), (-3, -1), (1, 1), (-1, -1))):
                    put(("t", at, i), z_raw(chunk * s), rt.at[at], zdev(to * s))

            def zjoin(i=i, k=k, z_own=z_own, rt=rt, st=st, s=s, fold=fold, zlead=zlead):
                need_own(k)
                for at in range(3):
                    copies[("t", at, i)].wait_recv()
                fold(st.at[0], [rt.at[0], rt.at[1], z_own(2 * s)], *zlead)
                put(("t", 5, i), st.at[0], rt.at[5], zdev(2 * s))
                fold(st.at[1], [rt.at[2], z_own(-2 * s)], *zlead)
                put(("t", 6, i), st.at[1], rt.at[6], zdev(-2 * s))

            def zmeet(i=i, k=k, z_own=z_own, rt=rt, fold=fold, zlead=zlead, dst=agg if yfirst else mid):
                need_own(k)
                for at in range(3, 7):
                    copies[("t", at, i)].wait_recv()
                fold(dst, [z_own(0)] + [rt.at[at] for at in range(3, 7)], *zlead)

            if yform == "c":
                event(("y0", i), y0, yk, after=ybase,
                      sends=[(("y1", i), yl[1], ysize), (("y3", i), yl[-1], ysize)])
                event(("y1", i), y1, yr - 1, needs=[("y1", i)], sends=[(("y2", i), yl[1], ysize)], cost=0.1 + FOLD * ysize * 2)
                event(("yd", i), y2, yr - 2, needs=[("y2", i), ("y3", i)], cost=0.1 + FOLD * ysize * 3)
            else:
                event(("y0", i), ystart, yk, after=ybase,
                      sends=[(("y+", i), yl[1], 2 * ysize), (("y-", i), yl[-1], 2 * ysize)])
                event(("yd", i), yend, yr - 2, needs=[("y+", i), ("y-", i)], cost=0.1 + FOLD * ysize * 4)
            if zform == "t":
                event(("z0", i), zpairs, zk, after=zbase,
                      sends=[(("t+", i), zl[1], 3 * zsize), (("t-", i), zl[-1], zsize),
                             (("T+", i), zl[1], zsize), (("T-", i), zl[-1], zsize)])
                event(("z1", i), zjoin, zr - 1, needs=[("t+", i), ("t-", i)],
                      sends=[(("u+", i), zl[1], 2 * zsize), (("u-", i), zl[-1], 2 * zsize)], cost=0.2 + FOLD * zsize * 5)
                event(("zd", i), zmeet, zr - 2, needs=[("u+", i), ("u-", i), ("T+", i), ("T-", i)],
                      cost=0.1 + FOLD * zsize * 5)
            if zform == "d":
                event(("z0", i), zflood, zk, after=zbase,
                      sends=[(("z+", i), zl[1], 8 * zsize), (("z-", i), zl[-1], 8 * zsize)])
                event(("zd", i), zsink, zr - 2, needs=[("z+", i), ("z-", i)], cost=0.1 + FOLD * zsize * 8)

            def zstart(i=i, z_raw=z_raw, rza=rza, rzb=rzb, s=s):
                put(("a", 0, i), z_raw(half * s), rza.at[0], zdev(s))
                put(("b", 0, i), z_raw(-(half - 1) * s), rzb.at[0], zdev(-s))

            if zform == "c":
                event(("z0", i), zstart, zk, after=zbase,
                      sends=[(("a", 0, i), zl[1], zsize), (("b", 0, i), zl[-1], zsize)])
                for h in range(1, half):
                    def za(i=i, k=k, h=h, z_own=z_own, rza=rza, sza=sza, s=s, fold=fold, zlead=zlead):
                        need_own(k)
                        copies[("a", h - 1, i)].wait_recv()
                        fold(sza.at[h - 1], [rza.at[h - 1], z_own((half - h) * s)], *zlead)
                        put(("a", h, i), sza.at[h - 1], rza.at[h], zdev(s))

                    event(("za", h, i), za, zr - 1, needs=[("a", h - 1, i)], sends=[(("a", h, i), zl[1], zsize)],
                          cost=0.1 + FOLD * zsize * 2)
                for h in range(1, half - 1):
                    def zb(i=i, k=k, h=h, z_own=z_own, rzb=rzb, szb=szb, s=s, fold=fold, zlead=zlead):
                        need_own(k)
                        copies[("b", h - 1, i)].wait_recv()
                        fold(szb.at[h - 1], [rzb.at[h - 1], z_own(-(half - 1 - h) * s)], *zlead)
                        put(("b", h, i), szb.at[h - 1], rzb.at[h], zdev(-s))

                    event(("zb", h, i), zb, zr - 1, needs=[("b", h - 1, i)], sends=[(("b", h, i), zl[-1], zsize)],
                          cost=0.1 + FOLD * zsize * 2)

                def zend(i=i, k=k, z_own=z_own, rza=rza, rzb=rzb, fold=fold, zlead=zlead,
                         dst=agg if yfirst else mid):
                    need_own(k)
                    copies[("a", half - 1, i)].wait_recv()
                    copies[("b", half - 2, i)].wait_recv()
                    fold(dst, [rza.at[half - 1], rzb.at[half - 2], z_own(0)], *zlead)

                event(("zd", i), zend, zr - 2, needs=[("a", half - 1, i), ("b", half - 2, i)],
                      cost=0.1 + FOLD * zsize * 3)
            finals[k].append(("zd", i) if yfirst else ("yd", i))

        def block_of(device):
            found = jnp.int32(0)
            for j in range(nb_all):
                found = jnp.where(owners_ref[0, j] == device, j, found)
            return found

        def peer(o):
            dz, dy = o // NY, o % NY
            step = jnp.where(dz % 2 == 1, (dz + 1) // 2, nz - dz // 2)
            return lax.rem(z + step, nz) * NY + lax.rem(y + dy, NY)

        for k, (c0, w, _) in enumerate(ROUNDS):
            kib = strip * w * 2 / 1024

            def route(k=k):
                agg, stage, grad = (buf[(n, k)] for n in ("agg", "stage", "grad"))

                def one(o, _):
                    to = peer(o)
                    stage[o] = agg[block_of(to)]
                    pltpu.make_async_remote_copy(
                        src_ref=stage.at[o], dst_ref=grad.at[me], send_sem=a2a_send.at[k], recv_sem=a2a_recv.at[k],
                        device_id=(to, ten), device_id_type=MESH,
                    ).start()
                    return 0

                lax.fori_loop(1, n_dp, one, 0)
                grad[me] = agg[block_of(me)]

            event(("route", k), route, k * 10 - 3, after=finals[k],
                  sends=[(("rz", q, k), ("z", q), kib * 8 * NY) for q in (1, -1)]
                  + [(("ry", q, k), ("y", q), kib * 2 * nz) for q in (1, -1)], cost=1.7)

        def a2a_all(sem, ref):
            part = ref.at[pl.ds(0, n_dp - 1)]
            return pltpu.make_async_copy(part, part, sem)

        waited = []

        def land(k):
            a2a_all(a2a_recv.at[k], buf[("grad", k)]).wait()
            if not waited:
                waited.append(k)
                for c in loads:
                    c.wait()
            w = ROUNDS[k][1]
            gk = buf[("grad", k)][...].reshape(width, w)
            buf["half"][:, ROUNDS[k][0]:ROUNDS[k][0] + w] = jnp.dot(
                buf["lroot"][...], gk, preferred_element_type=F32).astype(BF16)
            gf = gk.astype(F32)
            folded = jnp.sum((gf * gf).reshape(width // 8, 8, w), axis=0)
            buf["gsq"][k] = sum(folded[:, c:c + 128] for c in range(0, w, 128))

        for k in range(n_rounds):
            event(("land", k), functools.partial(land, k), k * 10 - 4,
                  needs=[("rz", q, k) for q in (1, -1)] + [("ry", q, k) for q in (1, -1)], cost=0.7)

        for c in own_copies:
            c.start()
        greet()
        order, _ = plan(events, *MODEL)
        started = False
        for e in order:
            if not started and (e["needs"] or e is order[-1]):
                started = True
                for c in loads:
                    c.start()
            e["emit"]()


        def whole():
            parts = [buf[("grad", k)][...].reshape(width, ROUNDS[k][1]) for k in range(n_rounds)]
            return parts[0] if len(parts) == 1 else jnp.concatenate(parts, axis=1)

        owned = jnp.int32(0)
        for j in range(nb_all):
            owned = owned + jnp.where(owners_ref[0, j] == me, 1, 0)
        mine = owned > 0
        tall = 128
        per = tall // strip
        pre, arrived = buf["pre"], buf["arrived"]

        def give(to):
            pltpu.make_async_remote_copy(
                src_ref=pre.at[to], dst_ref=arrived.at[me], send_sem=a2a_send.at[n_rounds],
                recv_sem=a2a_recv.at[n_rounds], device_id=(to, ten), device_id_type=MESH,
            ).start()

        squares = jnp.zeros((8, width), F32)
        for i in range(width // tall):
            rows = pl.ds(i * tall, tall)
            p = jnp.dot(buf["half"][rows, :], buf["rroot"][...], preferred_element_type=F32)
            pre[pl.ds(i * per, per)] = p.astype(BF16).reshape(per, strip, width)
            squares = squares + jnp.sum((p * p).reshape(tall // 8, 8, width), axis=0)
        arrived[me] = pre[me]

        grad_squares = jnp.sum(buf["gsq"][...], axis=0)
        count = width * width
        grad_mean = jnp.sum(grad_squares, axis=(0, 1), keepdims=True) / count
        pre_mean = jnp.sum(squares, axis=(0, 1), keepdims=True) / count
        factor = jnp.sqrt(grad_mean + epsilon) / jnp.sqrt(pre_mean + epsilon)
        share = (pre_mean / (pre_mean + epsilon)) * (grad_mean + epsilon) * count
        owned, block = jnp.int32(0), jnp.int32(0)
        for j in range(nb_all):
            here = owners_ref[0, j] == me
            owned = owned + jnp.where(here, 1, 0)
            block = jnp.where(here, j, block)
        mine = owned > 0
        share = lax.select(mine, share, jnp.zeros_like(share))
        factor = lax.select(mine, factor, jnp.zeros_like(factor))

        def exchange(ref, n, dev, at, value):
            ref[0] = value
            for o in range(1, n):
                pltpu.make_async_remote_copy(
                    src_ref=ref.at[0], dst_ref=ref.at[o], send_sem=sum_send.at[at], recv_sem=sum_recv.at[at],
                    device_id=dev(o), device_id_type=MESH,
                ).start()

            def finish():
                if n > 1:
                    part = ref.at[pl.ds(1, n - 1)]
                    pltpu.make_async_copy(part, part, sum_recv.at[at]).wait()
                return jnp.sum(ref[...], axis=0)

            return finish

        finish = exchange(buf["sum_t"], n_tensor, lambda o: (me, lax.rem(ten + o, n_tensor)), 0,
                          jnp.broadcast_to(share, (8, 128)))
        def give_to(spans):
            for first, last in spans:
                lax.fori_loop(first, last, lambda o, _: (give(peer(o)), 0)[1], 0)

        give_to(FIRST)

        lanes = lax.broadcasted_iota(jnp.int32, (8, 128), 1)
        in_row = lax.broadcasted_iota(jnp.int32, (8, 128), 0) == block
        local = jnp.where(lanes < 64, jnp.where(in_row, jnp.broadcast_to(factor, (8, 128)), 0.0), finish())
        finish = exchange(buf["sum_y"], NY, lambda o: (z * NY + lax.rem(y + o, NY), ten), 1, local)
        finish = exchange(buf["sum_z"], nz, lambda o: (lax.rem(z + o, nz) * NY + y, ten), 2, finish())
        give_to(LAST)

        gram_weight = (1.0 - decay_rate) / width

        def statistic(factor_ref, gram):
            add = gram_weight * gram
            add = lax.select(mine, add, jnp.zeros_like(add))
            return decay_rate * factor_ref + add

        grad = whole()
        flipped = grad.T
        buf["turned"][...] = flipped

        def left_rows(i, _):
            rows = pl.ds(i * tall, tall)
            gram = jnp.zeros((tall, width), F32)
            for k, (c0, w, _) in enumerate(ROUNDS):
                top = buf[("grad", k)][pl.ds(i * per, per)].reshape(tall, w)
                gram = gram + jnp.dot(top, buf["turned"][c0:c0 + w, :], preferred_element_type=F32)
            nl_ref[rows, :] = statistic(buf["lfac"][rows, :], gram)
            return 0

        lax.fori_loop(0, width // tall, left_rows, 0)
        def right_rows(i, _):
            rows = pl.ds(i * tall, tall)
            for k, (c0, w, _) in enumerate(ROUNDS):
                gram = jnp.dot(buf["turned"][rows, :], buf[("grad", k)][...].reshape(width, w), preferred_element_type=F32)
                nr_ref[rows, c0:c0 + w] = statistic(buf["rfac"][rows, c0:c0 + w], gram)
            return 0

        lax.fori_loop(0, width // tall, right_rows, 0)
        for c in copies.values():
            c.wait_send()
        for k in range(n_rounds):
            a2a_all(a2a_send.at[k], buf[("stage", k)]).wait()

        entries = nb_all * n_tensor * width * width
        norms = finish()
        scale = 1.0 / jnp.sqrt(norms[0:1, 64:65] / entries + epsilon)
        for at, (n, ref) in enumerate(((n_tensor, buf["sum_t"]), (NY, buf["sum_y"]), (nz, buf["sum_z"]))):
            if n > 1:
                part = ref.at[pl.ds(1, n - 1)]
                pltpu.make_async_copy(part, part, sum_send.at[at]).wait()
        scale = jnp.broadcast_to(scale, (strip, width))
        a2a_all(a2a_recv.at[n_rounds], arrived).wait()
        for j in range(nb_all):
            shaped = arrived[owners_ref[0, j]].astype(F32) * jnp.broadcast_to(norms[j:j + 1, 0:1], (strip, width))
            dir_ref[j] = (shaped * scale).astype(BF16)
        a2a_all(a2a_send.at[n_rounds], pre).wait()

    hbm = pl.BlockSpec(memory_space=pl.ANY)
    vmem = pl.BlockSpec(memory_space=pltpu.VMEM)
    new_left, new_right, directions = pl.pallas_call(
        kernel,
        out_shape=(
            pltpu.VMEM((width, width), F32),
            pltpu.VMEM((width, width), F32),
            pltpu.VMEM((nb_all, strip, width), BF16),
        ),
        in_specs=[pl.BlockSpec(memory_space=pltpu.SMEM)] + [hbm] * 5,
        out_specs=(vmem, vmem, vmem),
        scratch_shapes=shapes
        + [
            pltpu.SemaphoreType.DMA((n_msg,)),
            pltpu.SemaphoreType.DMA((n_msg,)),
            pltpu.SemaphoreType.DMA((n_rounds,)),
            pltpu.SemaphoreType.DMA((4,)),
            pltpu.SemaphoreType.DMA((n_rounds + 1,)),
            pltpu.SemaphoreType.DMA((n_rounds + 1,)),
            pltpu.SemaphoreType.DMA((3,)),
            pltpu.SemaphoreType.DMA((3,)),
        ],
        compiler_params=pltpu.CompilerParams(
            collective_id=0, has_side_effects=True, vmem_limit_bytes=58 * 1024 * 1024
        ),
        name="shampoo",
    )(owners, g, left_factor[0, 0], right_factor[0, 0], left_root[0, 0], right_root[0, 0])
    return new_left[None, None], new_right[None, None], directions


def solution(mesh):
    nz = mesh.shape["dp"] // NY
    return jax.shard_map(
        functools.partial(per_device, nz, mesh.shape["tensor"]),
        mesh=mesh,
        in_specs=(
            P("dp", "tensor", None, None),
            P("tensor", None),
            P("tensor", "dp", None, None),
            P("tensor", "dp", None, None),
            P("tensor", "dp", None, None),
            P("tensor", "dp", None, None),
        ),
        out_specs=(
            P("tensor", "dp", None, None),
            P("tensor", "dp", None, None),
            P("tensor", "dp", None),
        ),
        check_vma=False,
    )
```

```python
import functools

import jax
import jax.numpy as jnp
from jax import lax
from jax.experimental import pallas as pl
from jax.experimental.pallas import tpu as pltpu
from jax.sharding import PartitionSpec as P

MESH = pl.DeviceIdType.MESH
F32 = jnp.float32
BF16 = jnp.bfloat16
decay_rate = 0.95
epsilon = 1e-06
NY = 4

ROUNDS = (
    (0, 256, (
        (1, "y", 1, "cd", -6.07),
        (3, "y", -1, "ct", 8.4),
        (3, "y", 1, "ct", 11.2),
        (1, "z", 1, "cd", -6.03),
    )),
    (256, 128, (
        (3, "z", -1, "cd", 19.4),
        (5, "z", 1, "cd", 12.9),
    )),
    (384, 128, (
        (5, "z", -1, "cd", 25.3),
        (1, "y", -1, "cd", 13.09),
        (2, "y", -1, "cd", 19.2),
    )),
)
FIRST = ((4, 32),)
LAST = ((1, 4),)
FULL = False
FOLD = 0.002
YFAR = (1, -1, 2)
ZFAR = (1, -1, 2, -2, 3, -3, 4)
MODEL = (47.5, 2.0, 3.0)


class Whole:
    def __init__(self, ref, send, recv):
        self.ref, self.send, self.recv = ref, send, recv

    def wait_recv(self):
        pltpu.make_async_copy(self.ref, self.ref, self.recv).wait()

    def wait_send(self):
        pltpu.make_async_copy(self.ref, self.ref, self.send).wait()


def plan(events, rate, latency, lead):
    free = dict.fromkeys([(a, q) for a in "yz" for q in (1, -1)], 0.0)
    arrive, done, order, now = {}, {}, [], 0.0
    left = list(events)
    while left:
        best = None
        for e in left:
            if any(m not in arrive for m in e["needs"]) or any(d not in done for d in e["after"]):
                continue
            ready = max([arrive[m] for m in e["needs"]] + [now])
            if not e["needs"] and not e["after"]:
                ready = max([now] + [free[link] - lead for _, link, _ in e["sends"]])
            key = (ready, e["rank"])
            if best is None or key < best[0]:
                best = (key, e)
        (ready, _), e = best
        now = ready + e["cost"]
        for name, link, kib in e["sends"]:
            free[link] = max(free[link], now) + kib * 1.024 / rate
            arrive[name] = free[link] + latency
        done[e["name"]] = now
        order.append(e)
        left.remove(e)
    return order, now


def per_device(nz, n_tensor, gradients, owners, left_factor, right_factor, left_root, right_root):
    nb_all, width = gradients.shape[1], gradients.shape[2]
    n_dp = nz * NY
    strip = width // n_dp
    g = gradients.reshape(nb_all, nz, NY, strip, width)
    sets = []
    for k, (c0, w, found) in enumerate(ROUNDS):
        b0 = 0
        for nb, axis, s, forms, rank in found:
            sets.append((k, c0, w, b0, nb, axis == "y", s, (forms, rank)))
            b0 += nb
    names, shapes = [], []

    def buffer(name, shape, dtype=BF16):
        names.append(name)
        shapes.append(pltpu.VMEM(shape, dtype))

    messages = {}
    half = nz // 2
    for i, (k, c0, w, b0, nb, yfirst, s, forms) in enumerate(sets):
        ychunk = (nb, nz, strip, w) if yfirst else (nb, strip, w)
        zchunk = (nb, strip, w) if yfirst else (nb, NY, strip, w)
        forms = forms[0]
        yform, zform = forms if yfirst else forms[::-1]
        buffer(("mid", i), ychunk if yfirst else zchunk)
        if yform == "c":
            for n in ("ry1", "ry2", "ry3", "sy"):
                buffer((n, i), ychunk)
            found = [("y1",), ("y2",), ("y3",)]
        else:
            buffer(("ry", i), (NY - 1,) + ychunk)
            found = [("y",)]
        if zform == "c":
            buffer(("rza", i), (half,) + zchunk)
            buffer(("rzb", i), (half - 1,) + zchunk)
            buffer(("sza", i), (half - 1,) + zchunk)
            buffer(("szb", i), (half - 2,) + zchunk)
            found += [("a", h) for h in range(half)] + [("b", h) for h in range(half - 1)]
        elif zform == "t":
            buffer(("rt", i), (7,) + zchunk)
            buffer(("st", i), (2,) + zchunk)
            found += [("t", h) for h in range(7)]
        else:
            buffer(("rz", i), (nz - 1,) + zchunk)
            found += [("z",)]
        for n in found:
            messages[n + (i,)] = len(messages)
    for k, (c0, w, _) in enumerate(ROUNDS):
        buffer(("agg", k), (nb_all, strip, w))
        buffer(("stage", k), (n_dp, strip, w))
        buffer(("grad", k), (n_dp, strip, w))
    buffer("own", (nb_all, nz, NY, strip, width))
    buffer("lroot", (width, width))
    buffer("rroot", (width, width))
    buffer("lfac", (width, width), F32)
    buffer("rfac", (width, width), F32)
    buffer("pre", (n_dp, strip, width))
    buffer("half", (width, width))
    buffer("turned", (width, width))
    buffer("gsq", (len(ROUNDS), 8, 128), F32)
    buffer("arrived", (n_dp, strip, width))
    buffer("sum_t", (n_tensor, 8, 128), F32)
    buffer("sum_y", (NY, 8, 128), F32)
    buffer("sum_z", (nz, 8, 128), F32)

    n_msg = len(messages)
    n_rounds = len(ROUNDS)

    def kernel(owners_ref, g_ref, lf_ref, rf_ref, lr_ref, rr_ref, nl_ref, nr_ref, dir_ref, *scratch):
        buf = dict(zip(names, scratch))
        send, recv, own_sem, load_sem, a2a_send, a2a_recv, sum_send, sum_recv = scratch[len(names):]
        me, ten = lax.axis_index("dp"), lax.axis_index("tensor")
        z, y = me // NY, me % NY

        def zat(d):
            return lax.rem(z + d + 2 * nz, nz)

        def yat(d):
            return lax.rem(y + d + 2 * NY, NY)

        def zdev(d):
            return (zat(d) * NY + y, ten)

        def ydev(d):
            return (z * NY + yat(d), ten)

        barrier = pltpu.get_barrier_semaphore()

        met = [ydev(d) for d in (1, -1, 2)] + [zdev(d) for d in (1, -1, 2, -2, 3, -3, 4)]
        met += [(me, lax.rem(ten + o, n_tensor)) for o in range(1, n_tensor)]
        if FULL:
            met += [(zat(dz) * NY + yat(dy), ten) for dz in range(1, nz) for dy in range(1, NY)]

        def greet():
            for dev in met:
                pl.semaphore_signal(barrier, inc=1, device_id=dev, device_id_type=MESH)
            pl.semaphore_wait(barrier, len(met))

        own_copies = []
        for k, (c0, w, _) in enumerate(ROUNDS):
            cols = pl.ds(c0, w)
            own_copies.append(
                pltpu.make_async_copy(
                    g_ref.at[:, :, :, :, cols], buf["own"].at[:, :, :, :, cols], own_sem.at[k]
                )
            )
        loads = [
            pltpu.make_async_copy(lr_ref, buf["lroot"], load_sem.at[0]),
            pltpu.make_async_copy(rr_ref, buf["rroot"], load_sem.at[1]),
            pltpu.make_async_copy(lf_ref, buf["lfac"], load_sem.at[2]),
            pltpu.make_async_copy(rf_ref, buf["rfac"], load_sem.at[3]),
        ]
        copies = {}

        def put(name, src, dst, dev):
            i = messages[name]
            copies[name] = pltpu.make_async_remote_copy(
                src_ref=src, dst_ref=dst, send_sem=send.at[i], recv_sem=recv.at[i],
                device_id=dev, device_id_type=MESH,
            )
            copies[name].start()

        def total(parts):
            if len(parts) == 2:
                return parts[0] + parts[1]
            acc = parts[0].astype(F32)
            for p in parts[1:]:
                acc = acc + p.astype(F32)
            return acc.astype(BF16)

        events = []

        def event(name, emit, rank, needs=(), after=(), sends=(), cost=0.2):
            events.append(dict(name=name, emit=emit, rank=rank, needs=needs, after=after, sends=sends, cost=cost))

        loaded = set()

        def need_own(k):
            if k not in loaded:
                loaded.add(k)
                own_copies[k].wait()

        finals = {k: [] for k in range(n_rounds)}
        for i, (k, c0, w, b0, nb, yfirst, s, forms) in enumerate(sets):
            forms, rank = forms
            yform, zform = forms if yfirst else forms[::-1]
            cols = pl.ds(c0, w)
            blocks = pl.ds(b0, nb)
            kib = nb * strip * w * 2 / 1024

            def own_y(src, i=i, blocks=blocks, cols=cols, yfirst=yfirst):
                return (lambda d: src.at[blocks, :, yat(d), :, cols]) if yfirst else (lambda d: src.at[:, yat(d)])

            def own_z(src, i=i, blocks=blocks, cols=cols, yfirst=yfirst):
                return (lambda d: src.at[:, zat(d)]) if yfirst else (lambda d: src.at[blocks, zat(d), :, :, cols])

            def fold(dst, parts, lead, n_lead, nb=nb):
                if not lead:
                    for b in range(nb):
                        dst[b] = total([p[b] for p in parts])
                    return

                def one(v, _):
                    for b in range(nb):
                        dst[b, v] = total([p[b, v] for p in parts])
                    return 0

                lax.fori_loop(0, n_lead, one, 0)

            first_y, first_z = yfirst, not yfirst
            ysize = kib * nz if yfirst else kib
            zsize = kib if yfirst else kib * NY
            mid = buf[("mid", i)]
            y_raw = own_y(g_ref if yfirst else mid)
            y_own = own_y(buf["own"] if yfirst else mid)
            z_raw = own_z(mid if yfirst else g_ref)
            z_own = own_z(mid if yfirst else buf["own"])
            agg = buf[("agg", k)].at[blocks]
            ry1, ry2, ry3, sy = (buf.get((n, i)) for n in ("ry1", "ry2", "ry3", "sy"))
            rza, rzb, sza, szb = (buf.get((n, i)) for n in ("rza", "rzb", "sza", "szb"))
            ry, rz = buf.get(("ry", i)), buf.get(("rz", i))
            rt, st = buf.get(("rt", i)), buf.get(("st", i))
            ylead = (yfirst, nz)
            zlead = (not yfirst, NY)
            up, down = s, -s
            yl, zl = {1: ("y", s), -1: ("y", -s)}, {1: ("z", s), -1: ("z", -s)}
            yk, zk = (rank, k * 10 + 5) if yfirst else (k * 10 + 5, rank)
            yr, zr = (k * 10, zk) if yfirst else (yk, k * 10)
            ybase = () if yfirst else (("zd", i),)
            zbase = (("yd", i),) if yfirst else ()

            def y0(i=i, y_raw=y_raw, ry1=ry1, ry3=ry3, s=s):
                put(("y1", i), y_raw(2 * s), ry1, ydev(s))
                put(("y3", i), y_raw(-s), ry3, ydev(-s))

            def y1(i=i, k=k, y_own=y_own, ry1=ry1, ry2=ry2, sy=sy, s=s, fold=fold, ylead=ylead):
                need_own(k)
                copies[("y1", i)].wait_recv()
                fold(sy, [ry1, y_own(s)], *ylead)
                put(("y2", i), sy, ry2, ydev(s))

            def y2(i=i, k=k, y_own=y_own, ry2=ry2, ry3=ry3, fold=fold, ylead=ylead,
                   dst=mid if yfirst else agg):
                need_own(k)
                copies[("y2", i)].wait_recv()
                copies[("y3", i)].wait_recv()
                fold(dst, [ry2, ry3, y_own(0)], *ylead)

            def straight(name, raw, into, far, dev):
                i = messages[name]
                for at, d in enumerate(far):
                    pltpu.make_async_remote_copy(
                        src_ref=raw(d), dst_ref=into.at[at], send_sem=send.at[i], recv_sem=recv.at[i],
                        device_id=dev(d), device_id_type=MESH,
                    ).start()
                copies[name] = Whole(into, send.at[i], recv.at[i])

            def ystart(i=i, y_raw=y_raw, ry=ry, straight=straight):
                straight(("y", i), y_raw, ry, YFAR, ydev)

            def yend(i=i, k=k, y_own=y_own, ry=ry, fold=fold, ylead=ylead, dst=mid if yfirst else agg):
                need_own(k)
                copies[("y", i)].wait_recv()
                fold(dst, [y_own(0)] + [ry.at[at] for at in range(NY - 1)], *ylead)

            def zflood(i=i, z_raw=z_raw, rz=rz, straight=straight):
                straight(("z", i), z_raw, rz, ZFAR, zdev)

            def zsink(i=i, k=k, z_own=z_own, rz=rz, fold=fold, zlead=zlead, dst=agg if yfirst else mid):
                need_own(k)
                copies[("z", i)].wait_recv()
                fold(dst, [z_own(0)] + [rz.at[at] for at in range(nz - 1)], *zlead)

            def zpairs(i=i, z_raw=z_raw, rt=rt, s=s):
                for at, (chunk, to) in enumerate(((4, 2), (3, 1), (-3, -1), (1, 1), (-1, -1))):
                    put(("t", at, i), z_raw(chunk * s), rt.at[at], zdev(to * s))

            def zjoin(i=i, k=k, z_own=z_own, rt=rt, st=st, s=s, fold=fold, zlead=zlead):
                need_own(k)
                for at in range(3):
                    copies[("t", at, i)].wait_recv()
                fold(st.at[0], [rt.at[0], rt.at[1], z_own(2 * s)], *zlead)
                put(("t", 5, i), st.at[0], rt.at[5], zdev(2 * s))
                fold(st.at[1], [rt.at[2], z_own(-2 * s)], *zlead)
                put(("t", 6, i), st.at[1], rt.at[6], zdev(-2 * s))

            def zmeet(i=i, k=k, z_own=z_own, rt=rt, fold=fold, zlead=zlead, dst=agg if yfirst else mid):
                need_own(k)
                for at in range(3, 7):
                    copies[("t", at, i)].wait_recv()
                fold(dst, [z_own(0)] + [rt.at[at] for at in range(3, 7)], *zlead)

            if yform == "c":
                event(("y0", i), y0, yk, after=ybase,
                      sends=[(("y1", i), yl[1], ysize), (("y3", i), yl[-1], ysize)])
                event(("y1", i), y1, yr - 1, needs=[("y1", i)], sends=[(("y2", i), yl[1], ysize)], cost=0.1 + FOLD * ysize * 2)
                event(("yd", i), y2, yr - 2, needs=[("y2", i), ("y3", i)], cost=0.1 + FOLD * ysize * 3)
            else:
                event(("y0", i), ystart, yk, after=ybase,
                      sends=[(("y+", i), yl[1], 2 * ysize), (("y-", i), yl[-1], 2 * ysize)])
                event(("yd", i), yend, yr - 2, needs=[("y+", i), ("y-", i)], cost=0.1 + FOLD * ysize * 4)
            if zform == "t":
                event(("z0", i), zpairs, zk, after=zbase,
                      sends=[(("t+", i), zl[1], 3 * zsize), (("t-", i), zl[-1], zsize),
                             (("T+", i), zl[1], zsize), (("T-", i), zl[-1], zsize)])
                event(("z1", i), zjoin, zr - 1, needs=[("t+", i), ("t-", i)],
                      sends=[(("u+", i), zl[1], 2 * zsize), (("u-", i), zl[-1], 2 * zsize)], cost=0.2 + FOLD * zsize * 5)
                event(("zd", i), zmeet, zr - 2, needs=[("u+", i), ("u-", i), ("T+", i), ("T-", i)],
                      cost=0.1 + FOLD * zsize * 5)
            if zform == "d":
                event(("z0", i), zflood, zk, after=zbase,
                      sends=[(("z+", i), zl[1], 8 * zsize), (("z-", i), zl[-1], 8 * zsize)])
                event(("zd", i), zsink, zr - 2, needs=[("z+", i), ("z-", i)], cost=0.1 + FOLD * zsize * 8)

            def zstart(i=i, z_raw=z_raw, rza=rza, rzb=rzb, s=s):
                put(("a", 0, i), z_raw(half * s), rza.at[0], zdev(s))
                put(("b", 0, i), z_raw(-(half - 1) * s), rzb.at[0], zdev(-s))

            if zform == "c":
                event(("z0", i), zstart, zk, after=zbase,
                      sends=[(("a", 0, i), zl[1], zsize), (("b", 0, i), zl[-1], zsize)])
                for h in range(1, half):
                    def za(i=i, k=k, h=h, z_own=z_own, rza=rza, sza=sza, s=s, fold=fold, zlead=zlead):
                        need_own(k)
                        copies[("a", h - 1, i)].wait_recv()
                        fold(sza.at[h - 1], [rza.at[h - 1], z_own((half - h) * s)], *zlead)
                        put(("a", h, i), sza.at[h - 1], rza.at[h], zdev(s))

                    event(("za", h, i), za, zr - 1, needs=[("a", h - 1, i)], sends=[(("a", h, i), zl[1], zsize)],
                          cost=0.1 + FOLD * zsize * 2)
                for h in range(1, half - 1):
                    def zb(i=i, k=k, h=h, z_own=z_own, rzb=rzb, szb=szb, s=s, fold=fold, zlead=zlead):
                        need_own(k)
                        copies[("b", h - 1, i)].wait_recv()
                        fold(szb.at[h - 1], [rzb.at[h - 1], z_own(-(half - 1 - h) * s)], *zlead)
                        put(("b", h, i), szb.at[h - 1], rzb.at[h], zdev(-s))

                    event(("zb", h, i), zb, zr - 1, needs=[("b", h - 1, i)], sends=[(("b", h, i), zl[-1], zsize)],
                          cost=0.1 + FOLD * zsize * 2)

                def zend(i=i, k=k, z_own=z_own, rza=rza, rzb=rzb, fold=fold, zlead=zlead,
                         dst=agg if yfirst else mid):
                    need_own(k)
                    copies[("a", half - 1, i)].wait_recv()
                    copies[("b", half - 2, i)].wait_recv()
                    fold(dst, [rza.at[half - 1], rzb.at[half - 2], z_own(0)], *zlead)

                event(("zd", i), zend, zr - 2, needs=[("a", half - 1, i), ("b", half - 2, i)],
                      cost=0.1 + FOLD * zsize * 3)
            finals[k].append(("zd", i) if yfirst else ("yd", i))

        def block_of(device):
            found = jnp.int32(0)
            for j in range(nb_all):
                found = jnp.where(owners_ref[0, j] == device, j, found)
            return found

        def peer(o):
            dz, dy = o // NY, o % NY
            step = jnp.where(dz % 2 == 1, (dz + 1) // 2, nz - dz // 2)
            return lax.rem(z + step, nz) * NY + lax.rem(y + dy, NY)

        for k, (c0, w, _) in enumerate(ROUNDS):
            kib = strip * w * 2 / 1024

            def route(k=k):
                agg, stage, grad = (buf[(n, k)] for n in ("agg", "stage", "grad"))

                def one(o, _):
                    to = peer(o)
                    stage[o] = agg[block_of(to)]
                    pltpu.make_async_remote_copy(
                        src_ref=stage.at[o], dst_ref=grad.at[me], send_sem=a2a_send.at[k], recv_sem=a2a_recv.at[k],
                        device_id=(to, ten), device_id_type=MESH,
                    ).start()
                    return 0

                lax.fori_loop(1, n_dp, one, 0)
                grad[me] = agg[block_of(me)]

            event(("route", k), route, k * 10 - 3, after=finals[k],
                  sends=[(("rz", q, k), ("z", q), kib * 8 * NY) for q in (1, -1)]
                  + [(("ry", q, k), ("y", q), kib * 2 * nz) for q in (1, -1)], cost=1.7)

        def a2a_all(sem, ref):
            part = ref.at[pl.ds(0, n_dp - 1)]
            return pltpu.make_async_copy(part, part, sem)

        waited = []

        def land(k):
            a2a_all(a2a_recv.at[k], buf[("grad", k)]).wait()
            if not waited:
                waited.append(k)
                for c in loads:
                    c.wait()
            w = ROUNDS[k][1]
            gk = buf[("grad", k)][...].reshape(width, w)
            buf["half"][:, ROUNDS[k][0]:ROUNDS[k][0] + w] = jnp.dot(
                buf["lroot"][...], gk, preferred_element_type=F32).astype(BF16)
            gf = gk.astype(F32)
            folded = jnp.sum((gf * gf).reshape(width // 8, 8, w), axis=0)
            buf["gsq"][k] = sum(folded[:, c:c + 128] for c in range(0, w, 128))

        for k in range(n_rounds):
            event(("land", k), functools.partial(land, k), k * 10 - 4,
                  needs=[("rz", q, k) for q in (1, -1)] + [("ry", q, k) for q in (1, -1)], cost=0.7)

        greet()
        for c in own_copies:
            c.start()
        order, _ = plan(events, *MODEL)
        started = False
        for e in order:
            if not started and (e["needs"] or e is order[-1]):
                started = True
                for c in loads:
                    c.start()
            e["emit"]()


        def whole():
            parts = [buf[("grad", k)][...].reshape(width, ROUNDS[k][1]) for k in range(n_rounds)]
            return parts[0] if len(parts) == 1 else jnp.concatenate(parts, axis=1)

        owned = jnp.int32(0)
        for j in range(nb_all):
            owned = owned + jnp.where(owners_ref[0, j] == me, 1, 0)
        mine = owned > 0
        tall = 128
        per = tall // strip
        pre, arrived = buf["pre"], buf["arrived"]

        def give(to):
            pltpu.make_async_remote_copy(
                src_ref=pre.at[to], dst_ref=arrived.at[me], send_sem=a2a_send.at[n_rounds],
                recv_sem=a2a_recv.at[n_rounds], device_id=(to, ten), device_id_type=MESH,
            ).start()

        squares = jnp.zeros((8, width), F32)
        for i in range(width // tall):
            rows = pl.ds(i * tall, tall)
            p = jnp.dot(buf["half"][rows, :], buf["rroot"][...], preferred_element_type=F32)
            pre[pl.ds(i * per, per)] = p.astype(BF16).reshape(per, strip, width)
            squares = squares + jnp.sum((p * p).reshape(tall // 8, 8, width), axis=0)
        arrived[me] = pre[me]

        grad_squares = jnp.sum(buf["gsq"][...], axis=0)
        count = width * width
        grad_mean = jnp.sum(grad_squares, axis=(0, 1), keepdims=True) / count
        pre_mean = jnp.sum(squares, axis=(0, 1), keepdims=True) / count
        factor = jnp.sqrt(grad_mean + epsilon) / jnp.sqrt(pre_mean + epsilon)
        share = (pre_mean / (pre_mean + epsilon)) * (grad_mean + epsilon) * count
        owned, block = jnp.int32(0), jnp.int32(0)
        for j in range(nb_all):
            here = owners_ref[0, j] == me
            owned = owned + jnp.where(here, 1, 0)
            block = jnp.where(here, j, block)
        mine = owned > 0
        share = lax.select(mine, share, jnp.zeros_like(share))
        factor = lax.select(mine, factor, jnp.zeros_like(factor))

        def exchange(ref, n, dev, at, value):
            ref[0] = value
            for o in range(1, n):
                pltpu.make_async_remote_copy(
                    src_ref=ref.at[0], dst_ref=ref.at[o], send_sem=sum_send.at[at], recv_sem=sum_recv.at[at],
                    device_id=dev(o), device_id_type=MESH,
                ).start()

            def finish():
                if n > 1:
                    part = ref.at[pl.ds(1, n - 1)]
                    pltpu.make_async_copy(part, part, sum_recv.at[at]).wait()
                return jnp.sum(ref[...], axis=0)

            return finish

        finish = exchange(buf["sum_t"], n_tensor, lambda o: (me, lax.rem(ten + o, n_tensor)), 0,
                          jnp.broadcast_to(share, (8, 128)))
        def give_to(spans):
            for first, last in spans:
                lax.fori_loop(first, last, lambda o, _: (give(peer(o)), 0)[1], 0)

        give_to(FIRST)

        lanes = lax.broadcasted_iota(jnp.int32, (8, 128), 1)
        in_row = lax.broadcasted_iota(jnp.int32, (8, 128), 0) == block
        local = jnp.where(lanes < 64, jnp.where(in_row, jnp.broadcast_to(factor, (8, 128)), 0.0), finish())
        finish = exchange(buf["sum_y"], NY, lambda o: (z * NY + lax.rem(y + o, NY), ten), 1, local)
        finish = exchange(buf["sum_z"], nz, lambda o: (lax.rem(z + o, nz) * NY + y, ten), 2, finish())
        give_to(LAST)

        gram_weight = (1.0 - decay_rate) / width

        def statistic(factor_ref, gram):
            add = gram_weight * gram
            add = lax.select(mine, add, jnp.zeros_like(add))
            return decay_rate * factor_ref + add

        grad = whole()
        flipped = grad.T
        buf["turned"][...] = flipped

        def left_rows(i, _):
            rows = pl.ds(i * tall, tall)
            gram = jnp.zeros((tall, width), F32)
            for k, (c0, w, _) in enumerate(ROUNDS):
                top = buf[("grad", k)][pl.ds(i * per, per)].reshape(tall, w)
                gram = gram + jnp.dot(top, buf["turned"][c0:c0 + w, :], preferred_element_type=F32)
            nl_ref[rows, :] = statistic(buf["lfac"][rows, :], gram)
            return 0

        lax.fori_loop(0, width // tall, left_rows, 0)
        def right_rows(i, _):
            rows = pl.ds(i * tall, tall)
            for k, (c0, w, _) in enumerate(ROUNDS):
                gram = jnp.dot(buf["turned"][rows, :], buf[("grad", k)][...].reshape(width, w), preferred_element_type=F32)
                nr_ref[rows, c0:c0 + w] = statistic(buf["rfac"][rows, c0:c0 + w], gram)
            return 0

        lax.fori_loop(0, width // tall, right_rows, 0)
        for c in copies.values():
            c.wait_send()
        for k in range(n_rounds):
            a2a_all(a2a_send.at[k], buf[("stage", k)]).wait()

        entries = nb_all * n_tensor * width * width
        norms = finish()
        scale = 1.0 / jnp.sqrt(norms[0:1, 64:65] / entries + epsilon)
        for at, (n, ref) in enumerate(((n_tensor, buf["sum_t"]), (NY, buf["sum_y"]), (nz, buf["sum_z"]))):
            if n > 1:
                part = ref.at[pl.ds(1, n - 1)]
                pltpu.make_async_copy(part, part, sum_send.at[at]).wait()
        scale = jnp.broadcast_to(scale, (strip, width))
        a2a_all(a2a_recv.at[n_rounds], arrived).wait()
        for j in range(nb_all):
            shaped = arrived[owners_ref[0, j]].astype(F32) * jnp.broadcast_to(norms[j:j + 1, 0:1], (strip, width))
            dir_ref[j] = (shaped * scale).astype(BF16)
        a2a_all(a2a_send.at[n_rounds], pre).wait()

    hbm = pl.BlockSpec(memory_space=pl.ANY)
    vmem = pl.BlockSpec(memory_space=pltpu.VMEM)
    new_left, new_right, directions = pl.pallas_call(
        kernel,
        out_shape=(
            pltpu.VMEM((width, width), F32),
            pltpu.VMEM((width, width), F32),
            pltpu.VMEM((nb_all, strip, width), BF16),
        ),
        in_specs=[pl.BlockSpec(memory_space=pltpu.SMEM)] + [hbm] * 5,
        out_specs=(vmem, vmem, vmem),
        scratch_shapes=shapes
        + [
            pltpu.SemaphoreType.DMA((n_msg,)),
            pltpu.SemaphoreType.DMA((n_msg,)),
            pltpu.SemaphoreType.DMA((n_rounds,)),
            pltpu.SemaphoreType.DMA((4,)),
            pltpu.SemaphoreType.DMA((n_rounds + 1,)),
            pltpu.SemaphoreType.DMA((n_rounds + 1,)),
            pltpu.SemaphoreType.DMA((3,)),
            pltpu.SemaphoreType.DMA((3,)),
        ],
        compiler_params=pltpu.CompilerParams(
            collective_id=0, has_side_effects=True, vmem_limit_bytes=58 * 1024 * 1024
        ),
        name="shampoo",
    )(owners, g, left_factor[0, 0], right_factor[0, 0], left_root[0, 0], right_root[0, 0])
    return new_left[None, None], new_right[None, None], directions


def solution(mesh):
    nz = mesh.shape["dp"] // NY
    return jax.shard_map(
        functools.partial(per_device, nz, mesh.shape["tensor"]),
        mesh=mesh,
        in_specs=(
            P("dp", "tensor", None, None),
            P("tensor", None),
            P("tensor", "dp", None, None),
            P("tensor", "dp", None, None),
            P("tensor", "dp", None, None),
            P("tensor", "dp", None, None),
        ),
        out_specs=(
            P("tensor", "dp", None, None),
            P("tensor", "dp", None, None),
            P("tensor", "dp", None),
        ),
        check_vma=False,
    )
```
